32 devices in a mesh: seq: 16 (over z, y, x), head: 2 (over core).
Axes of the slice: x: 2, y: 2, z: 4, core: 2. Of those that a mesh axis runs over, the one named last changes fastest.
Arguments:
- queries: bfloat16 [1, 2048, 2048], P(None, 'seq', 'head'), may hold values from -6 to 6
- keys: bfloat16 [1, 2048, 2048], P(None, 'seq', 'head'), may hold values from -8 to 8
- values: bfloat16 [1, 2048, 4096], P(None, 'seq', 'head'), may hold values from -12 to 12
- out_gate: bfloat16 [1, 2048, 4096], P(None, 'seq', 'head'), may hold values from -6 to 6
- log_decay: float32 [1, 32, 2048], P(None, 'head', 'seq'), may hold values from -0.7 to 0
- beta: float32 [1, 32, 2048], P(None, 'head', 'seq'), may hold values from 0 to 0.9
- norm_gain: float32 [128], replicated, may hold values from 0.5 to 1.5
- out_weight: bfloat16 [4096, 2048], P('head'), may hold values from -0.09375 to 0.09375
- owner: int32 [1, 32], P(None, 'head'), may hold values from 0 to 15, as said below
Outputs:
- layer_output: bfloat16 [2048, 1, 2048], P(('seq', 'head'))
- decode_states: float32 [16, 32, 128, 128], P('seq', 'head')
The draws below stay inside these ranges and needn't reach their ends.
Inputs may be any that keep to these rules, and one draw needn't show every extreme that they name: For every value head h, owner[s, h] = (owner[0, h] + s * 16) modulo 16, so the prompts of one head have different owners.
All inputs are finite; a program needn't handle non-finite values.
Results may differ from the reference program's by a relative error of at most 0.006.
Values may be sent and summed in bfloat16 or wider, within the bound.
No kernel may reach another device: no remote copies, remote signals or barrier semaphores. Data moves between devices by JAX's collectives and lax.ppermute only.
A program may use at most 128 MiB of HBM per device.

```python
import math
import jax
import jax.numpy as jnp
from jax import lax

D = 2048
VALUE_HEADS_TOTAL = 32
HK = 16
DK = 128
DV = 128
BLOCK_TOKENS = 64
NUMBER_OF_PROMPTS = 1
TOK_DEV = 128
TOKENS_PER_PROMPT = 2048
N_SEQ = 16
N_HEAD = 2


def head_kinds(key):
    shuffled = jax.random.permutation(jax.random.fold_in(key, 7), VALUE_HEADS_TOTAL)
    share = VALUE_HEADS_TOTAL // 4
    fast_heads = shuffled < share
    pulsed_heads = jnp.logical_and(shuffled >= share, shuffled < 2 * share)
    return (fast_heads, pulsed_heads)


def draw_keys(key, part):
    key = jax.random.fold_in(key, 31)
    reshape_every_block = (NUMBER_OF_PROMPTS, TOKENS_PER_PROMPT, HK * DK)
    own_part = jax.random.normal(jax.random.fold_in(key, 1), reshape_every_block, jnp.float32)
    shared_part = jax.random.normal(jax.random.fold_in(key, 2), (NUMBER_OF_PROMPTS, 1, HK * DK), jnp.float32)
    mixed = own_part + shared_part
    return jnp.clip(mixed, -8.0, 8.0).astype(jnp.bfloat16)


def draw_log_decay(key, part):
    fast_heads, pulsed_heads = head_kinds(key)
    seq_devices = TOKENS_PER_PROMPT // TOK_DEV
    base_fast = -1.0 / jax.random.uniform(jax.random.fold_in(key, 1), (VALUE_HEADS_TOTAL,), jnp.float32, 30.0, 50.0)
    spread_slow = jnp.exp(jax.random.uniform(jax.random.fold_in(key, 2), (VALUE_HEADS_TOTAL,), jnp.float32, math.log(0.2), 0.0))
    base_slow = -0.5 * spread_slow / TOKENS_PER_PROMPT
    roughness = jnp.exp(jax.random.uniform(jax.random.fold_in(key, 3), (NUMBER_OF_PROMPTS, VALUE_HEADS_TOTAL, TOKENS_PER_PROMPT), jnp.float32, -math.log(2.0), math.log(2.0)))
    blocks = jnp.exp(jax.random.uniform(jax.random.fold_in(key, 4), (NUMBER_OF_PROMPTS, VALUE_HEADS_TOTAL, seq_devices, 1), jnp.float32, -math.log(2.0), math.log(2.0)))
    blocks = jnp.broadcast_to(blocks, (NUMBER_OF_PROMPTS, VALUE_HEADS_TOTAL, seq_devices, TOK_DEV)).reshape(NUMBER_OF_PROMPTS, VALUE_HEADS_TOTAL, TOKENS_PER_PROMPT)
    fast_rate = base_fast[None, :, None] * roughness * blocks
    slow_rate = base_slow[None, :, None] * roughness * blocks
    shard_ids = jnp.arange(seq_devices, dtype=jnp.int32)
    pulse_offset = jax.random.randint(jax.random.fold_in(key, 10), (NUMBER_OF_PROMPTS, VALUE_HEADS_TOTAL, 1), 0, 3)
    pulse_shard = (shard_ids[None, None, :] + pulse_offset) % 3 == 2
    pulse_loss = jax.random.uniform(jax.random.fold_in(key, 11), (NUMBER_OF_PROMPTS, VALUE_HEADS_TOTAL, seq_devices), jnp.float32, 1.2, 2.0)
    pulse_shard = jnp.broadcast_to(pulse_shard[..., None], (NUMBER_OF_PROMPTS, VALUE_HEADS_TOTAL, seq_devices, TOK_DEV)).reshape(NUMBER_OF_PROMPTS, VALUE_HEADS_TOTAL, TOKENS_PER_PROMPT)
    pulse_loss = jnp.broadcast_to(pulse_loss[..., None], (NUMBER_OF_PROMPTS, VALUE_HEADS_TOTAL, seq_devices, TOK_DEV)).reshape(NUMBER_OF_PROMPTS, VALUE_HEADS_TOTAL, TOKENS_PER_PROMPT)
    pulsed_rate = jnp.where(pulse_shard, -pulse_loss / TOK_DEV * roughness, slow_rate)
    decay_rate_entries = jnp.where(fast_heads[None, :, None], fast_rate, jnp.where(pulsed_heads[None, :, None], pulsed_rate, slow_rate))
    surge_locations = jax.random.randint(jax.random.fold_in(key, 5), (NUMBER_OF_PROMPTS, VALUE_HEADS_TOTAL, 2), 0, TOKENS_PER_PROMPT)
    surge_extent = jnp.log(jax.random.uniform(jax.random.fold_in(key, 6), (NUMBER_OF_PROMPTS, VALUE_HEADS_TOTAL, 2), jnp.float32, 0.6, 0.85))
    position_list = jnp.arange(TOKENS_PER_PROMPT, dtype=jnp.int32)[None, None, None, :] == surge_locations[..., None]
    surge_events = jnp.sum(jnp.where(position_list, surge_extent[..., None], 0.0), axis=2)
    return jnp.maximum(decay_rate_entries + surge_events, -0.7).astype(jnp.float32)


def draw_beta(key, part):
    fast_heads, pulsed_heads = head_kinds(key)
    reshape_every_block = (NUMBER_OF_PROMPTS, VALUE_HEADS_TOTAL, TOKENS_PER_PROMPT)
    fast_values = jax.random.uniform(jax.random.fold_in(key, 8), reshape_every_block, jnp.float32, 0.2, 0.9)
    slow_factor = jnp.exp(jax.random.uniform(jax.random.fold_in(key, 9), reshape_every_block, jnp.float32, math.log(0.25), math.log(2.5)))
    gradual_value_rows = 1.0 * DK / TOKENS_PER_PROMPT * slow_factor
    block_index_list = jnp.arange(TOKENS_PER_PROMPT, dtype=jnp.int32) // BLOCK_TOKENS
    spike_block_tokens = jax.random.randint(jax.random.fold_in(key, 12), (NUMBER_OF_PROMPTS, VALUE_HEADS_TOTAL, 1), 0, TOKENS_PER_PROMPT // BLOCK_TOKENS)
    inside_spike = block_index_list[None, None, :] == spike_block_tokens
    spike_value_rows = jax.random.uniform(jax.random.fold_in(key, 13), reshape_every_block, jnp.float32, 0.5, 0.9)
    drawn_value_rows = jnp.where(inside_spike, spike_value_rows, gradual_value_rows)
    return jnp.where(fast_heads[None, :, None], fast_values, drawn_value_rows).astype(jnp.float32)


def draw_owner(key, part):
    seq_devices = TOKENS_PER_PROMPT // TOK_DEV
    first_owner = jax.random.randint(jax.random.fold_in(key, 21), (VALUE_HEADS_TOTAL,), 0, seq_devices)
    chosen_head = jax.random.randint(jax.random.fold_in(key, 22), (), 0, VALUE_HEADS_TOTAL)
    head_ids = jnp.arange(VALUE_HEADS_TOTAL, dtype=jnp.int32)
    forced_owners = [seq_devices - 1, 0, seq_devices // 2, seq_devices // 2 - 1, 1, seq_devices - 2]
    for offset_index in range(len(forced_owners)):
        first_owner = jnp.where(head_ids == (chosen_head + offset_index) % VALUE_HEADS_TOTAL, forced_owners[offset_index], first_owner)
    request_ids = jnp.arange(NUMBER_OF_PROMPTS, dtype=jnp.int32)[:, None] * (seq_devices // NUMBER_OF_PROMPTS)
    return ((first_owner[None, :] + request_ids) % seq_devices).astype(jnp.int32)


def level_of(rng, dims, shards, smallest, largest):
    def one(axis_at, blocks):
        draws = jax.random.uniform(jax.random.fold_in(jax.random.fold_in(rng, 6), axis_at), (blocks,), jnp.float32, smallest / len(shards), largest / len(shards))
        return jnp.repeat(jnp.exp(draws), dims[axis_at] // blocks).reshape((-1,) + (1,) * (len(dims) - axis_at - 1))

    level = one(*shards[0])
    for cut in shards[1:]:
        level = level * one(*cut)
    return level


def normal_values(own_key, shape, width, limit, cuts=(), kind=jnp.bfloat16):
    entries = jax.random.normal(own_key, shape, jnp.float32) * width
    if len(cuts) > 0:
        entries = level_of(own_key, shape, cuts, -0.22, 0.18) * entries
    return jnp.clip(entries, min=-limit, max=limit).astype(kind)


def setup_inputs(seed: int = 0) -> dict:
    key_list = jax.random.split(jax.random.key(seed), 10)
    return {
        "queries": normal_values(key_list[0], (NUMBER_OF_PROMPTS, TOKENS_PER_PROMPT, HK * DK), 1.0, 6.0, ((1, 16), (2, 2))),
        "keys": draw_keys(jax.random.fold_in(key_list[9], 71), 0),
        "values": normal_values(key_list[2], (NUMBER_OF_PROMPTS, TOKENS_PER_PROMPT, VALUE_HEADS_TOTAL * DV), 2.0, 12.0, ((1, 16), (2, 2))),
        "out_gate": normal_values(key_list[3], (NUMBER_OF_PROMPTS, TOKENS_PER_PROMPT, VALUE_HEADS_TOTAL * DV), 1.0, 6.0, ((1, 16), (2, 2))),
        "log_decay": draw_log_decay(jax.random.fold_in(key_list[9], 71), 0),
        "beta": draw_beta(jax.random.fold_in(key_list[9], 71), 0),
        "norm_gain": jnp.clip(1.0 + 0.1 * jax.random.normal(key_list[6], (DV,), jnp.float32), 0.5, 1.5),
        "out_weight": normal_values(key_list[7], (VALUE_HEADS_TOTAL * DV, D), (VALUE_HEADS_TOTAL * DV) ** -0.5, 0.09375, ((0, 2),)),
        "owner": draw_owner(jax.random.fold_in(key_list[9], 71), 0),
    }


PRECISE = lax.Precision.HIGHEST

def unit_rows(tensor, head_count, head_width):
    floats = tensor.astype(jnp.float32).reshape(tensor.shape[0], tensor.shape[1], head_count, head_width)
    return floats * lax.rsqrt(lax.optimization_barrier(jnp.sum(floats * floats, axis=-1, keepdims=True)) + 1e-06)

def to_spans(tensor, repeat):
    widened = jnp.repeat(tensor, repeat, axis=2)
    shaped = widened.reshape(widened.shape[0], widened.shape[1] // BLOCK_TOKENS, BLOCK_TOKENS, widened.shape[2], widened.shape[3])
    return jnp.transpose(shaped, (1, 0, 3, 2, 4))

def gate_spans(tensor):
    shaped = tensor.reshape(tensor.shape[0], tensor.shape[1], tensor.shape[2] // BLOCK_TOKENS, BLOCK_TOKENS)
    return jnp.transpose(shaped, (2, 0, 1, 3))

def prepare(query_span, key_span, value_span, gate_span, beta_span):
    span_size = gate_span.shape[-1]
    cumulative = jnp.cumsum(gate_span, axis=-1)
    row_ids = lax.broadcasted_iota(jnp.int32, (span_size, span_size), 0)
    col_ids = lax.broadcasted_iota(jnp.int32, (span_size, span_size), 1)
    lower_mask = row_ids >= col_ids
    strict_mask = row_ids > col_ids
    log_gaps = jnp.where(lower_mask, cumulative[..., :, None] - cumulative[..., None, :], 0.0)
    decay_matrix = jnp.where(lower_mask, jnp.exp(log_gaps), 0.0)
    key_products = jnp.einsum('...td,...id->...ti', key_span, key_span, precision=PRECISE)
    system = jnp.where(strict_mask, beta_span[..., :, None] * decay_matrix * key_products, 0.0)
    system = system + jnp.eye(span_size, dtype=jnp.float32)
    scaled = jnp.exp(cumulative)[..., None]
    right_side = beta_span[..., None] * jnp.concatenate([value_span, scaled * key_span], axis=-1)
    solved = lax.linalg.triangular_solve(system, right_side, left_side=True, lower=True, unit_diagonal=True)
    update = solved[..., :value_span.shape[-1]]
    erasers = solved[..., value_span.shape[-1]:]
    mixing = decay_matrix * jnp.einsum('...td,...id->...ti', query_span, key_span, precision=PRECISE)
    tail_keys = jnp.exp(cumulative[..., -1:] - cumulative)[..., None] * key_span
    return (cumulative, update, erasers, mixing, tail_keys)

def advance(state_now, cumulative, update, erasers, mixing, tail_keys, query_span):
    fresh_values = update - jnp.einsum('...ck,...kv->...cv', erasers, state_now, precision=PRECISE)
    output = jnp.exp(cumulative)[..., None] * jnp.einsum('...ck,...kv->...cv', query_span, state_now, precision=PRECISE)
    output = output + jnp.einsum('...ti,...iv->...tv', mixing, fresh_values, precision=PRECISE)
    last_decay = jnp.exp(cumulative[..., -1])[..., None, None]
    state_after = last_decay * state_now + jnp.einsum('...ck,...cv->...kv', tail_keys, fresh_values, precision=PRECISE)
    return (state_after, output)

def reference(queries, keys, values, out_gate, log_decay, beta, norm_gain, out_weight, owner):
    length = queries.shape[1]
    repeat = VALUE_HEADS_TOTAL // HK
    query_all = to_spans(unit_rows(queries, HK, DK) * DK ** (-0.5), repeat)
    key_all = to_spans(unit_rows(keys, HK, DK), repeat)
    value_all = to_spans(values.astype(jnp.float32).reshape(NUMBER_OF_PROMPTS, length, VALUE_HEADS_TOTAL, DV), 1)
    gate_all = gate_spans(log_decay)
    beta_all = gate_spans(beta)

    def span_step(state_now, pieces):
        query_span, key_span, value_span, gate_span, beta_span = pieces
        cumulative, update, erasers, mixing, tail_keys = prepare(query_span, key_span, value_span, gate_span, beta_span)
        return advance(state_now, cumulative, update, erasers, mixing, tail_keys, query_span)
    zero_state = jnp.zeros((NUMBER_OF_PROMPTS, VALUE_HEADS_TOTAL, DK, DV), jnp.float32)
    final_state, outputs = lax.scan(span_step, zero_state, (query_all, key_all, value_all, gate_all, beta_all))
    readout = jnp.transpose(outputs, (1, 0, 3, 2, 4)).reshape(NUMBER_OF_PROMPTS, length, VALUE_HEADS_TOTAL, DV)
    gate_values = out_gate.astype(jnp.float32).reshape(NUMBER_OF_PROMPTS, length, VALUE_HEADS_TOTAL, DV)
    normed = readout * lax.rsqrt(lax.optimization_barrier(jnp.mean(readout * readout, axis=-1, keepdims=True)) + 1e-06) * norm_gain * jax.nn.silu(gate_values)
    normed = normed.astype(jnp.bfloat16)
    flattened = normed.reshape(NUMBER_OF_PROMPTS * length, VALUE_HEADS_TOTAL * DV)
    group_width = VALUE_HEADS_TOTAL * DV // N_HEAD

    def add_group(group_index, running):
        block_rows = lax.dynamic_slice_in_dim(flattened, group_index * group_width, group_width, 1)
        weights = lax.dynamic_slice_in_dim(out_weight, group_index * group_width, group_width, 0)
        partial_value = jnp.dot(block_rows.astype(jnp.float32), weights.astype(jnp.float32), preferred_element_type=jnp.float32)
        rounded = lax.optimization_barrier(partial_value.astype(jnp.bfloat16))
        return running + rounded.astype(jnp.float32)
    running = lax.fori_loop(0, N_HEAD, add_group, jnp.zeros((NUMBER_OF_PROMPTS * length, D), jnp.float32))
    layer_output = jnp.transpose(running.reshape(NUMBER_OF_PROMPTS, length, D), (1, 0, 2)).astype(jnp.bfloat16)
    owned_mask = (owner[:, :, None] == jnp.arange(N_SEQ, dtype=jnp.int32)[None, None, :]).astype(jnp.float32)
    decode_states = jnp.einsum('shn,shkv->nhkv', owned_mask, final_state, precision=PRECISE)
    return (layer_output, decode_states)
```

```python
import functools

import jax
import jax.numpy as jnp
from jax import lax
from jax.experimental import pallas as pl
from jax.experimental.pallas import tpu as pltpu
from jax.sharding import PartitionSpec as P

DK = 128
DV = 128
SMALL = 16
HIGH = lax.Precision.HIGHEST
F32 = jnp.float32
BF16 = jnp.bfloat16
VMEM_LIMIT = 48 * 1024 * 1024

NN = (((1,), (0,)), ((), ()))
NT = (((1,), (1,)), ((), ()))
TN = (((0,), (0,)), ((), ()))


def dot(a, b, dims=NN, precision=None):
    return lax.dot_general(a, b, dims, precision=precision, preferred_element_type=F32)


def split(x):
    high = x.astype(BF16)
    return high, (x - high.astype(F32)).astype(BF16)


def dot3(a, b):
    a_high, a_low = a
    b_high, b_low = b
    return dot(a_high, b_high) + (dot(a_high, b_low) + dot(a_low, b_high))


def row_col(size):
    return (
        lax.broadcasted_iota(jnp.int32, (size, size), 0),
        lax.broadcasted_iota(jnp.int32, (size, size), 1),
    )


def maps_kernel(k_ref, v_ref, g_ref, b_ref, pair_ref, solved_ref, l_scr, d_scr, t_scr):
    tokens = k_ref.shape[1]
    heads = g_ref.shape[1]
    repeat = heads // (k_ref.shape[2] // DK)
    blocks = tokens // SMALL
    row, col = row_col(tokens)
    lower = row >= col
    strict = row > col
    eye = row == col
    same_small = (row // SMALL) == (col // SMALL)
    gates = g_ref[0]
    betas = b_ref[0]
    tri = jnp.where(lower, 1.0, 0.0)
    cum_cols = dot(tri, gates, NT, HIGH)
    cum_rows = dot(gates, tri, NT, HIGH)
    beta_cols = dot(jnp.where(eye, 1.0, 0.0), betas, NT, HIGH)
    pick = jnp.where(
        lax.broadcasted_iota(jnp.int32, (tokens, DK), 0) % SMALL
        == lax.broadcasted_iota(jnp.int32, (tokens, DK), 1),
        1.0,
        0.0,
    ).astype(BF16)
    unit = [
        jnp.where(
            lax.broadcasted_iota(jnp.int32, (blocks, tokens), 1)
            == lax.broadcasted_iota(jnp.int32, (blocks, tokens), 0) * SMALL + i,
            1.0,
            0.0,
        )
        for i in range(SMALL)
    ]
    systems = []
    key_cols, key_rows = [], []
    for h in range(heads):
        kh = h // repeat
        if h % repeat == 0:
            key = k_ref[0, :, kh * DK : (kh + 1) * DK]
            gram = dot(key, key, NT)
            on_diag = jnp.where(eye, gram, 0.0)
            key_cols.append(lax.rsqrt(jnp.sum(on_diag, axis=1, keepdims=True) + 1e-6))
            key_rows.append(lax.rsqrt(jnp.sum(on_diag, axis=0, keepdims=True) + 1e-6))
        decay = jnp.exp(jnp.where(strict, cum_cols[:, h : h + 1] - cum_rows[h : h + 1, :], -1e30))
        system = decay * gram * (beta_cols[:, h : h + 1] * key_cols[kh]) * key_rows[kh]
        systems.append(system)
        high, low = split(jnp.where(same_small, system, 0.0))
        d_scr[h] = dot(high, pick) + dot(low, pick)
    for h in range(heads):
        rows = [unit[0]]
        for i in range(1, SMALL):
            coef = d_scr[h, pl.ds(i, blocks, stride=SMALL), :]
            value = unit[i]
            for j in range(i):
                value = value - coef[:, j : j + 1] * rows[j]
            rows.append(value)
        for i in range(SMALL):
            t_scr[h, pl.ds(i, blocks, stride=SMALL), :] = rows[i]
    inverse = [t_scr[h] for h in range(heads)]
    size = SMALL
    while size < tokens:
        mask = jnp.logical_and((row // (2 * size)) == (col // (2 * size)), (row // size) != (col // size))
        parts = [split(t) for t in inverse]
        inner = [dot3(split(jnp.where(mask, systems[h], 0.0)), parts[h]) for h in range(heads)]
        inverse = [inverse[h] - dot3(parts[h], split(inner[h])) for h in range(heads)]
        size *= 2
    for h in range(heads):
        kh = h // repeat
        key = k_ref[0, :, kh * DK : (kh + 1) * DK]
        scaled = inverse[h] * betas[h : h + 1, :]
        update = dot(scaled.astype(BF16), v_ref[0, :, h * DV : (h + 1) * DV])
        erase = dot((scaled * (jnp.exp(cum_rows[h : h + 1, :]) * key_rows[kh])).astype(BF16), key)
        last = cum_rows[h : h + 1, tokens - 1 :]
        weight = jnp.exp(last - cum_cols[:, h : h + 1]) * key_cols[kh]
        both = jnp.concatenate([erase, update], axis=1)
        solved_ref[h] = both.astype(BF16)
        moved = dot(key, (both * weight).astype(BF16), TN)
        gone = moved[:, :DK] + jnp.where(eye[:DK, :DK], 1.0 - jnp.exp(last), 0.0)
        pair_ref[h] = jnp.concatenate([gone, moved[:, DK:]], axis=1).astype(BF16)


def mix_kernel(q_ref, k_ref, z_ref, g_ref, gain_ref, solved_ref, query_ref, intra_ref, gate_ref):
    tokens = k_ref.shape[1]
    heads = g_ref.shape[1]
    repeat = heads // (k_ref.shape[2] // DK)
    row, col = row_col(tokens)
    lower = row >= col
    eye = row == col
    gates = g_ref[0]
    tri = jnp.where(lower, 1.0, 0.0)
    cum_cols = dot(tri, gates, NT, HIGH)
    cum_rows = dot(gates, tri, NT, HIGH)
    gain = gain_ref[0:1, :]
    ones = jnp.ones((8, DK), BF16)
    for h in range(heads):
        kh = h // repeat
        if h % repeat == 0:
            key = k_ref[0, :, kh * DK : (kh + 1) * DK]
            query = q_ref[0, :, kh * DK : (kh + 1) * DK]
            keyf = key.astype(F32)
            square_high, square_low = split(keyf * keyf)
            key_row = lax.rsqrt((dot(ones, square_high, NT) + dot(ones, square_low, NT))[0:1] + 1e-6)
            queryf = query.astype(F32)
            query_col = lax.rsqrt(jnp.sum(queryf * queryf, axis=1, keepdims=True) + 1e-6) * DK**-0.5
            product = dot(query, key, NT) * query_col * key_row
        decay = jnp.exp(jnp.where(lower, cum_cols[:, h : h + 1] - cum_rows[h : h + 1, :], -1e30))
        mixed = dot((decay * product).astype(BF16), solved_ref[h])
        intra_ref[:, h * DV : (h + 1) * DV] = mixed[:, DK:]
        reach = jnp.exp(cum_cols[:, h : h + 1]) * query_col
        query_ref[:, h * DK : (h + 1) * DK] = (reach * queryf - mixed[:, :DK]).astype(BF16)
        z = z_ref[0, :, h * DV : (h + 1) * DV].astype(F32)
        gate_ref[:, h * DV : (h + 1) * DV] = gain * z / (1.0 + jnp.exp(-z))


def chain_kernel(pair_ref, start_ref, entry_ref, exit_ref):
    count, heads = pair_ref.shape[0], pair_ref.shape[1]
    states = [start_ref[h].astype(F32) for h in range(heads)]
    for j in range(count):
        for h in range(heads):
            high, low = split(states[h])
            entry_ref[j, h] = high
            moved = dot(pair_ref[j, h, :, :DK], jnp.concatenate([high, low], axis=1))
            states[h] = states[h] - (moved[:, :DV] + moved[:, DV:]) + pair_ref[j, h, :, DK:].astype(F32)
    for h in range(heads):
        exit_ref[h] = states[h].astype(BF16)


def read_kernel(query_ref, intra_ref, gate_ref, entry_ref, w_ref, out_ref, normed_scr):
    heads = entry_ref.shape[0]

    @pl.when(pl.program_id(0) == 0)
    def _():
        for h in range(heads):
            cols = slice(h * DV, (h + 1) * DV)
            value = intra_ref[:, cols] + dot(query_ref[:, cols], entry_ref[h])
            scale = lax.rsqrt(jnp.mean(value * value, axis=1, keepdims=True) + 1e-6)
            normed_scr[:, cols] = (value * scale * gate_ref[:, cols]).astype(BF16)

    out_ref[...] = dot(normed_scr[...], w_ref[...]).astype(BF16)


def params():
    return pltpu.CompilerParams(vmem_limit_bytes=VMEM_LIMIT)


def shard_maps(keys, values, log_decay, beta):
    tokens, heads, key_heads = keys.shape[1], log_decay.shape[1], keys.shape[2] // DK
    step = min(8, heads)
    key_step = step * key_heads // heads
    shape = jax.ShapeDtypeStruct((heads, tokens, DK + DV), BF16)
    pair = jax.ShapeDtypeStruct((heads, DK, DK + DV), BF16)
    return pl.pallas_call(
        maps_kernel,
        grid=(heads // step,),
        in_specs=[
            pl.BlockSpec((1, tokens, key_step * DK), lambda i: (0, 0, i)),
            pl.BlockSpec((1, tokens, step * DV), lambda i: (0, 0, i)),
            pl.BlockSpec((1, step, tokens), lambda i: (0, i, 0)),
            pl.BlockSpec((1, step, tokens), lambda i: (0, i, 0)),
        ],
        out_specs=[
            pl.BlockSpec((step, DK, DK + DV), lambda i: (i, 0, 0)),
            pl.BlockSpec((step, tokens, DK + DV), lambda i: (i, 0, 0)),
        ],
        out_shape=[pair, shape],
        scratch_shapes=[
            pltpu.VMEM((step, tokens, tokens), F32),
            pltpu.VMEM((step, tokens, DK), F32),
            pltpu.VMEM((step, tokens, tokens), F32),
        ],
        compiler_params=params(),
        name="shard_maps",
    )(keys, values, log_decay, beta)


def local_mix(queries, keys, out_gate, log_decay, gain, solved):
    tokens, heads, key_heads = keys.shape[1], log_decay.shape[1], keys.shape[2] // DK
    step = min(8, heads)
    key_step = step * key_heads // heads
    wide = pl.BlockSpec((tokens, step * DV), lambda i: (0, i))
    return pl.pallas_call(
        mix_kernel,
        grid=(heads // step,),
        in_specs=[
            pl.BlockSpec((1, tokens, key_step * DK), lambda i: (0, 0, i)),
            pl.BlockSpec((1, tokens, key_step * DK), lambda i: (0, 0, i)),
            pl.BlockSpec((1, tokens, step * DV), lambda i: (0, 0, i)),
            pl.BlockSpec((1, step, tokens), lambda i: (0, i, 0)),
            pl.BlockSpec((1, DV), lambda i: (0, 0)),
            pl.BlockSpec((step, tokens, DK + DV), lambda i: (i, 0, 0)),
        ],
        out_specs=[wide, wide, wide],
        out_shape=[
            jax.ShapeDtypeStruct((tokens, heads * DK), BF16),
            jax.ShapeDtypeStruct((tokens, heads * DV), F32),
            jax.ShapeDtypeStruct((tokens, heads * DV), F32),
        ],
        compiler_params=params(),
        cost_estimate=pl.CostEstimate(flops=heads * 10 * 128**3, bytes_accessed=4 << 20, transcendentals=0),
        name="local_mix",
    )(queries, keys, out_gate, log_decay, gain, solved)


def run_chain(pairs, start):
    count, heads = pairs.shape[0], pairs.shape[1]
    return pl.pallas_call(
        chain_kernel,
        out_shape=[
            jax.ShapeDtypeStruct((count, heads, DK, DV), BF16),
            jax.ShapeDtypeStruct((heads, DK, DV), BF16),
        ],
        compiler_params=params(),
        name="chain",
    )(pairs, start)


def read_out(query, intra, gate, entry, weight):
    tokens, width = query.shape
    columns = weight.shape[1]
    step = min(512, columns)
    whole = lambda i: (0, 0)
    return pl.pallas_call(
        read_kernel,
        grid=(columns // step,),
        in_specs=[
            pl.BlockSpec((tokens, width), whole),
            pl.BlockSpec((tokens, width), whole),
            pl.BlockSpec((tokens, width), whole),
            pl.BlockSpec(entry.shape, lambda i: (0, 0, 0)),
            pl.BlockSpec((width, step), lambda i: (0, i)),
        ],
        out_specs=pl.BlockSpec((tokens, step), lambda i: (0, i)),
        out_shape=jax.ShapeDtypeStruct((tokens, columns), BF16),
        scratch_shapes=[pltpu.VMEM((tokens, width), BF16)],
        compiler_params=params(),
        name="read_out",
    )(query, intra, gate, entry, weight)


def group_size(count, heads):
    return max(s for s in range(1, 9) if count % s == 0 and heads % s == 0)


def local(queries, keys, values, out_gate, log_decay, beta, norm_gain, out_weight, owner):
    tokens, heads = keys.shape[1], log_decay.shape[1]
    count = lax.axis_size("seq")
    me = lax.axis_index("seq")
    size = group_size(count, heads)
    groups = count // size
    own = heads // size
    members = [[g * size + i for i in range(size)] for g in range(groups)]

    def swap(x):
        return lax.all_to_all(x, "seq", 0, 0, axis_index_groups=members, tiled=True)

    def hop(x, source, target):
        return lax.ppermute(x, "seq", [(source * size + i, target * size + i) for i in range(size)])

    pair, solved = shard_maps(keys, values, log_decay, beta)
    pairs = swap(pair.reshape(size, own, DK, DK + DV))
    query, intra, gate = local_mix(queries, keys, out_gate, log_decay, norm_gain[None], solved)
    start = jnp.zeros((own, DK, DV), BF16)
    for g in range(groups - 1):
        _, leave = run_chain(pairs, start)
        start = start + hop(leave, g, g + 1)
    entries, leave = run_chain(pairs, start)
    entry = swap(entries).reshape(heads, DK, DV)
    last = jnp.where(me // size == groups - 1, leave, jnp.zeros_like(leave))
    for g in range(groups - 1, 0, -1):
        last = last + hop(last, g, g - 1)
    mine = lax.dynamic_slice_in_dim(owner[0], (me % size) * own, own)
    to = (me // size) * size + jnp.arange(size, dtype=jnp.int32)
    kept = (mine[None, :] == to[:, None])[:, :, None, None]
    finals = swap(jnp.where(kept, last[None], jnp.zeros_like(last)[None]))
    decode_states = finals.reshape(1, heads, DK, DV).astype(F32)
    partial_value = read_out(query, intra, gate, entry, out_weight)
    ranks = lax.axis_size("head")
    if ranks == 2:
        half = tokens // 2
        rank = lax.axis_index("head")
        keep = lax.dynamic_slice_in_dim(partial_value, rank * half, half)
        give = lax.dynamic_slice_in_dim(partial_value, (1 - rank) * half, half)
        got = lax.ppermute(give, "head", [(0, 1), (1, 0)])
        total = (keep.astype(F32) + got.astype(F32)).astype(BF16)
    else:
        total = lax.psum_scatter(partial_value, "head", scatter_dimension=0, tiled=True)
    return (total[:, None, :], decode_states)


def solution(mesh):
    placed = (
        P(None, "seq", "head"),
        P(None, "seq", "head"),
        P(None, "seq", "head"),
        P(None, "seq", "head"),
        P(None, "head", "seq"),
        P(None, "head", "seq"),
        P(),
        P("head", None),
        P(None, "head"),
    )
    return jax.shard_map(
        local,
        mesh=mesh,
        in_specs=placed,
        out_specs=(P(("seq", "head"), None, None), P("seq", "head", None, None)),
        check_vma=False,
    )
```

```python
import jax
import jax.numpy as jnp
from jax import lax
from jax.experimental import pallas as pl
from jax.experimental.pallas import tpu as pltpu
from jax.sharding import PartitionSpec as P

DK = 128
DV = 128
SMALL = 16
EXTRA = 16
HIGH = lax.Precision.HIGHEST
F32 = jnp.float32
BF16 = jnp.bfloat16
VMEM_LIMIT = 40 * 1024 * 1024
VMEM_MOST = 63 * 1024 * 1024
VMEM_WIDE = 50 * 1024 * 1024
VMEM_LEAST = 4 * 1024 * 1024

NN = (((1,), (0,)), ((), ()))
NT = (((1,), (1,)), ((), ()))
TN = (((0,), (0,)), ((), ()))


def dot(a, b, dims=NN, precision=None):
    return lax.dot_general(a, b, dims, precision=precision, preferred_element_type=F32)


def split(x):
    high = x.astype(BF16)
    return high, (x - high.astype(F32)).astype(BF16)


def dot3(a, b):
    width = b[0].shape[1]
    both = dot(a[0], jnp.concatenate(b, axis=1))
    return both[:, :width] + (both[:, width:] + dot(a[1], b[0]))


def row_col(size):
    return (
        lax.broadcasted_iota(jnp.int32, (size, size), 0),
        lax.broadcasted_iota(jnp.int32, (size, size), 1),
    )


def inverses(systems, d_scr, t_scr):
    count, tokens = len(systems), systems[0].shape[0]
    blocks = tokens // SMALL
    row, col = row_col(tokens)
    same_small = (row // SMALL) == (col // SMALL)
    pick = jnp.where((row % SMALL) == col, 1.0, 0.0).astype(BF16)
    lane = lax.broadcasted_iota(jnp.int32, (blocks, tokens), 1)
    first = lax.broadcasted_iota(jnp.int32, (blocks, tokens), 0) * SMALL
    unit = [jnp.where(lane == first + i, 1.0, 0.0) for i in range(SMALL)]
    for u in range(count):
        high, low = split(jnp.where(same_small, systems[u], 0.0))
        d_scr[u] = dot(high, pick) + dot(low, pick)
    for u in range(count):
        rows = [unit[0]]
        for i in range(1, SMALL):
            coef = d_scr[u, pl.ds(i, blocks, stride=SMALL), :]
            value = unit[i]
            for j in range(i):
                value = value - coef[:, j : j + 1] * rows[j]
            rows.append(value)
        for i in range(SMALL):
            t_scr[u, pl.ds(i, blocks, stride=SMALL), :] = rows[i]
    found = [t_scr[u] for u in range(count)]
    size = SMALL
    while 2 * size < tokens:
        mask = jnp.logical_and((row // (2 * size)) == (col // (2 * size)), (row // size) != (col // size))
        parts = [split(t) for t in found]
        inner = [dot3(split(jnp.where(mask, systems[u], 0.0)), parts[u]) for u in range(count)]
        found = [found[u] - dot3(parts[u], split(inner[u])) for u in range(count)]
        size *= 2
    upper = [split(t[:size, :size]) for t in found]
    lower = [split(t[size:, size:]) for t in found]
    inner = [dot3(split(systems[u][size:, :size]), upper[u]) for u in range(count)]
    corner = [dot3(lower[u], split(inner[u])) for u in range(count)]
    return [
        jnp.concatenate(
            [found[u][:size], jnp.concatenate([-corner[u], found[u][size:, size:]], axis=1)], axis=0
        )
        for u in range(count)
    ]


def norms(key, eye):
    gram = dot(key, key, NT)
    on_diag = jnp.where(eye, gram, 0.0)
    return (
        gram,
        lax.rsqrt(jnp.sum(on_diag, axis=1, keepdims=True) + 1e-6),
        lax.rsqrt(jnp.sum(on_diag, axis=0, keepdims=True) + 1e-6),
    )


def pack_kernel(k_ref, v_ref, g_ref, b_ref, out_ref, g_scr, b_scr, e_scr, sems):
    size = out_ref.shape[0]
    tokens, heads = g_ref.shape[2], g_ref.shape[1]
    own = heads // size
    repeat = heads // (k_ref.shape[2] // DK)
    keys = max(1, own // repeat)
    copies = [
        pltpu.make_async_copy(g_ref, g_scr, sems.at[0]),
        pltpu.make_async_copy(b_ref, b_scr, sems.at[1]),
    ]
    for d in range(size):
        for i in range(keys):
            kh = d * own // repeat + i
            copies.append(
                pltpu.make_async_copy(
                    k_ref.at[0, :, kh * DK : (kh + 1) * DK],
                    out_ref.at[d, i * tokens : (i + 1) * tokens],
                    sems.at[len(copies)],
                )
            )
        for i in range(own):
            h = d * own + i
            copies.append(
                pltpu.make_async_copy(
                    v_ref.at[0, :, h * DV : (h + 1) * DV],
                    out_ref.at[d, (keys + i) * tokens : (keys + i + 1) * tokens],
                    sems.at[len(copies)],
                )
            )
    for copy in copies:
        copy.start()
    copies[0].wait()
    copies[1].wait()
    e_scr[...] = jnp.zeros_like(e_scr)
    for which, scr in ((0, g_scr), (1, b_scr)):
        rest = scr[0]
        for part in range(3):
            piece = rest.astype(BF16).astype(F32)
            rest = rest - piece
            for d in range(size):
                at = part * 2 * own + which * own
                e_scr[d, at : at + own] = piece[d * own : (d + 1) * own]
    for d in range(size):
        out_ref[d, (keys + own) * tokens :] = e_scr[d].astype(BF16)
    for copy in copies[2:]:
        copy.wait()


def local_kernel(
    q_ref, k_ref, v_ref, z_ref, g_ref, b_ref, gain_ref, query_ref, intra_ref, gate_ref, d_scr, t_scr
):
    tokens = k_ref.shape[1]
    heads = g_ref.shape[1]
    repeat = heads // (k_ref.shape[2] // DK)
    row, col = row_col(tokens)
    lower = row >= col
    eye = row == col
    gates = g_ref[0]
    betas = b_ref[0]
    tri = jnp.where(lower, 1.0, 0.0)
    cum_cols = dot(tri, gates, NT, HIGH)
    cum_rows = dot(gates, tri, NT, HIGH)
    beta_cols = dot(jnp.where(eye, 1.0, 0.0), betas, NT, HIGH)
    gain = gain_ref[0:1, :]
    key_side = [norms(k_ref[0, :, i * DK : (i + 1) * DK], eye) for i in range(heads // repeat)]
    systems = []
    for h in range(heads):
        gram, key_col, key_row = key_side[h // repeat]
        decay = jnp.exp(jnp.where(row > col, cum_cols[:, h : h + 1] - cum_rows[h : h + 1, :], -1e30))
        systems.append(decay * gram * (beta_cols[:, h : h + 1] * key_col) * key_row)
    found = inverses(systems, d_scr, t_scr)
    for h in range(heads):
        kh = h // repeat
        _, key_col, key_row = key_side[kh]
        key = k_ref[0, :, kh * DK : (kh + 1) * DK]
        if h % repeat == 0:
            query = q_ref[0, :, kh * DK : (kh + 1) * DK]
            queryf = query.astype(F32)
            query_col = lax.rsqrt(jnp.sum(queryf * queryf, axis=1, keepdims=True) + 1e-6) * DK**-0.5
            product = dot(query, key, NT) * query_col * key_row
        scaled = found[h] * betas[h : h + 1, :]
        update = dot(scaled.astype(BF16), v_ref[0, :, h * DV : (h + 1) * DV])
        erase = dot((scaled * (jnp.exp(cum_rows[h : h + 1, :]) * key_row)).astype(BF16), key)
        both = jnp.concatenate([erase, update], axis=1).astype(BF16)
        decay = jnp.exp(jnp.where(lower, cum_cols[:, h : h + 1] - cum_rows[h : h + 1, :], -1e30))
        mixed = dot((decay * product).astype(BF16), both)
        intra_ref[:, h * DV : (h + 1) * DV] = mixed[:, DK:]
        reach = jnp.exp(cum_cols[:, h : h + 1]) * query_col
        query_ref[:, h * DK : (h + 1) * DK] = (reach * queryf - mixed[:, :DK]).astype(BF16)
        z = z_ref[0, :, h * DV : (h + 1) * DV].astype(F32)
        gate_ref[:, h * DV : (h + 1) * DV] = gain * z / (1.0 + jnp.exp(-z))


def group_kernel(own, keys, x_ref, move_ref, add_ref, pair_ref, y_scr, d_scr, t_scr):
    shards = x_ref.shape[0]
    tokens = DK
    repeat = own // keys
    row, col = row_col(tokens)
    lower = row >= col
    eye = row == col
    base = (keys + own) * tokens
    take_row = lax.broadcasted_iota(jnp.int32, (8, EXTRA), 0)
    take_col = lax.broadcasted_iota(jnp.int32, (8, EXTRA), 1)
    take = jnp.where(
        jnp.logical_and(take_col % (2 * own) == take_row, take_col < 6 * own), 1.0, 0.0
    ).astype(BF16)
    plain = jnp.concatenate([dot(take, x_ref[j, base : base + EXTRA]) for j in range(shards)], axis=0)
    tri = jnp.where(lower, 1.0, 0.0)
    cum_cols = dot(tri, plain, NT, HIGH)
    cum_rows = dot(plain, tri, NT, HIGH)
    plain_cols = dot(jnp.where(eye, 1.0, 0.0), plain, NT, HIGH)

    @pl.when(pl.program_id(0) == 0)
    def _():
        for h in range(own):
            y_scr[h] = jnp.concatenate(
                [jnp.where(eye, 1.0, 0.0), jnp.zeros((tokens, DV), F32)], axis=1
            )

    units = [(j, h) for j in range(shards) for h in range(own)]
    key_side = {}
    for j in range(shards):
        for i in range(keys):
            key_side[j, i] = norms(x_ref[j, i * tokens : (i + 1) * tokens], eye)
    systems = []
    for j, h in units:
        gram, key_col, key_row = key_side[j, h // repeat]
        at = j * 8 + h
        decay = jnp.exp(jnp.where(row > col, cum_cols[:, at : at + 1] - cum_rows[at : at + 1, :], -1e30))
        systems.append(decay * gram * (plain_cols[:, at + own : at + own + 1] * key_col) * key_row)
    found = inverses(systems, d_scr, t_scr)
    moved = {}
    for u, (j, h) in enumerate(units):
        i = h // repeat
        _, key_col, key_row = key_side[j, i]
        at = j * 8 + h
        key = x_ref[j, i * tokens : (i + 1) * tokens]
        value = x_ref[j, (keys + h) * tokens : (keys + h + 1) * tokens]
        scaled = found[u] * plain[at + own : at + own + 1, :]
        high, low = split(scaled)
        update = dot(high, value) + dot(low, value)
        high, low = split(scaled * (jnp.exp(cum_rows[at : at + 1, :]) * key_row))
        erase = dot(high, key) + dot(low, key)
        last = cum_rows[at : at + 1, tokens - 1 :]
        weight = jnp.exp(last - cum_cols[:, at : at + 1]) * key_col
        high, low = split(jnp.concatenate([erase, update], axis=1) * weight)
        both = dot(key, high, TN) + dot(key, low, TN)
        moved[j, h] = (jnp.where(eye, jnp.exp(last), 0.0) - both[:, :DK], both[:, DK:])
    total = [y_scr[h] for h in range(own)]
    for j in range(shards):
        for h in range(own):
            move_ref[j, h] = total[h][:, :DK].astype(BF16)
            add_ref[j, h] = total[h][:, DK:]
            gone = dot3(split(moved[j, h][0]), split(total[h]))
            total[h] = jnp.concatenate([gone[:, :DK], gone[:, DK:] + moved[j, h][1]], axis=1)
    for h in range(own):
        y_scr[h] = total[h]
        pair_ref[h] = total[h].astype(BF16)


def spread(start, final, info_ref, move_ref, add_ref, out_ref):
    size, own = move_ref.shape[0], move_ref.shape[1]
    for h in range(own):
        at = start[h].astype(BF16)
        to = info_ref[1 + h]
        for j in range(size):
            entry = dot(move_ref[j, h], at) + add_ref[j, h]
            kept = jnp.where(to == j, final[h], jnp.zeros_like(final[h]))
            out_ref[j, h] = jnp.concatenate([entry, kept], axis=1).astype(BF16)


def pair_spread_kernel(info_ref, move_ref, add_ref, mine_ref, got_ref, out_ref):
    own = mine_ref.shape[0]
    late = info_ref[0] == 1
    start, final = [], []
    for h in range(own):
        mine, got = mine_ref[h], got_ref[h]
        first = jnp.where(late, got[:, DK:].astype(F32), mine[:, DK:].astype(F32))
        second = jnp.where(late, mine.astype(F32), got.astype(F32))
        final.append(dot(second[:, :DK].astype(BF16), first.astype(BF16)) + second[:, DK:])
        start.append(jnp.where(late, first, jnp.zeros_like(first)))
    spread(start, final, info_ref, move_ref, add_ref, out_ref)


def spread_kernel(info_ref, move_ref, add_ref, start_ref, final_ref, out_ref):
    own = start_ref.shape[0]
    start = [start_ref[h].astype(F32) for h in range(own)]
    final = [final_ref[h].astype(F32) for h in range(own)]
    spread(start, final, info_ref, move_ref, add_ref, out_ref)


def read_kernel(back_ref, query_ref, intra_ref, gate_ref, w_ref, out_ref, q_scr, i_scr, z_scr, w_scr, normed_scr, sems):
    heads = back_ref.shape[0]
    pieces, step = w_scr.shape[0], w_scr.shape[2]
    copies = [
        pltpu.make_async_copy(query_ref, q_scr, sems.at[0]),
        pltpu.make_async_copy(intra_ref, i_scr, sems.at[1]),
        pltpu.make_async_copy(gate_ref, z_scr, sems.at[2]),
    ] + [
        pltpu.make_async_copy(w_ref.at[:, c * step : (c + 1) * step], w_scr.at[c], sems.at[3 + c])
        for c in range(pieces)
    ]
    for copy in copies:
        copy.start()
    for copy in copies[:3]:
        copy.wait()
    for h in range(heads):
        cols = slice(h * DV, (h + 1) * DV)
        value = i_scr[:, cols] + dot(q_scr[:, cols], back_ref[h, :, :DV])
        scale = lax.rsqrt(jnp.mean(value * value, axis=1, keepdims=True) + 1e-6)
        normed_scr[:, cols] = (value * scale * z_scr[:, cols]).astype(BF16)
    for c in range(pieces):
        copies[3 + c].wait()
        out_ref[:, c * step : (c + 1) * step] = dot(normed_scr[...], w_scr[c]).astype(BF16)


def cost(micros):
    return pl.CostEstimate(flops=int(micros * 1.15e9), bytes_accessed=1 << 20, transcendentals=0)


def params(limit=VMEM_LIMIT):
    return pltpu.CompilerParams(vmem_limit_bytes=limit)


def pack(keys, values, log_decay, beta, size):
    tokens, heads, key_heads = keys.shape[1], log_decay.shape[1], keys.shape[2] // DK
    own = heads // size
    carried = max(1, own * key_heads // heads)
    rows = (carried + own) * tokens + EXTRA
    far = pl.BlockSpec(memory_space=pltpu.HBM)
    return pl.pallas_call(
        pack_kernel,
        in_specs=[far, far, far, far],
        out_shape=jax.ShapeDtypeStruct((size, rows, DK), BF16),
        scratch_shapes=[
            pltpu.VMEM(log_decay.shape, F32),
            pltpu.VMEM(beta.shape, F32),
            pltpu.VMEM((size, EXTRA, tokens), F32),
            pltpu.SemaphoreType.DMA((2 + size * (carried + own),)),
        ],
        compiler_params=params(VMEM_MOST),
        cost_estimate=cost(2),
        name="pack",
    )(keys, values, log_decay, beta)


def local_part(queries, keys, values, out_gate, log_decay, beta, gain):
    tokens, heads, key_heads = keys.shape[1], log_decay.shape[1], keys.shape[2] // DK
    step = min(8, heads)
    key_step = step * key_heads // heads
    wide = pl.BlockSpec((tokens, step * DV), lambda i: (0, i))
    narrow = pl.BlockSpec((1, tokens, key_step * DK), lambda i: (0, 0, i))
    broad = pl.BlockSpec((1, tokens, step * DV), lambda i: (0, 0, i))
    thin = pl.BlockSpec((1, step, tokens), lambda i: (0, i, 0))
    return pl.pallas_call(
        local_kernel,
        grid=(heads // step,),
        in_specs=[narrow, narrow, broad, broad, thin, thin, pl.BlockSpec((1, DV), lambda i: (0, 0))],
        out_specs=[wide, wide, wide],
        out_shape=[
            jax.ShapeDtypeStruct((tokens, heads * DK), BF16),
            jax.ShapeDtypeStruct((tokens, heads * DV), F32),
            jax.ShapeDtypeStruct((tokens, heads * DV), F32),
        ],
        scratch_shapes=[pltpu.VMEM((step, tokens, DK), F32), pltpu.VMEM((step, tokens, tokens), F32)],
        compiler_params=params(VMEM_MOST),
        cost_estimate=cost(12),
        name="local_part",
    )(queries, keys, values, out_gate, log_decay, beta, gain)


def group_maps(x, own, keys):
    size, rows = x.shape[0], x.shape[1]
    step = min(4, size)
    block = lambda i: (i, 0, 0, 0)
    return pl.pallas_call(
        lambda *refs: group_kernel(own, keys, *refs),
        grid=(size // step,),
        in_specs=[pl.BlockSpec((step, rows, DK), lambda i: (i, 0, 0))],
        out_specs=[
            pl.BlockSpec((step, own, DK, DK), block),
            pl.BlockSpec((step, own, DK, DV), block),
            pl.BlockSpec((own, DK, DK + DV), lambda i: (0, 0, 0)),
        ],
        out_shape=[
            jax.ShapeDtypeStruct((size, own, DK, DK), BF16),
            jax.ShapeDtypeStruct((size, own, DK, DV), F32),
            jax.ShapeDtypeStruct((own, DK, DK + DV), BF16),
        ],
        scratch_shapes=[
            pltpu.VMEM((own, DK, DK + DV), F32),
            pltpu.VMEM((step * own, DK, DK), F32),
            pltpu.VMEM((step * own, DK, DK), F32),
        ],
        compiler_params=params(),
        cost_estimate=cost(12),
        name="group_maps",
    )(x)


def spread_states(kernel, info, move, add, one, two):
    near = pl.BlockSpec(memory_space=pltpu.VMEM)
    size, own = move.shape[0], move.shape[1]
    return pl.pallas_call(
        kernel,
        in_specs=[pl.BlockSpec(memory_space=pltpu.SMEM), near, near, near, near],
        out_shape=jax.ShapeDtypeStruct((size, own, DK, 2 * DV), BF16),
        compiler_params=params(),
        cost_estimate=cost(2),
        name="spread_states",
    )(info, move, add, one, two)


def read_out(query, intra, gate, back, weight):
    tokens, width = query.shape
    columns = weight.shape[1]
    pieces = 8
    near = pl.BlockSpec(memory_space=pltpu.VMEM)
    far = pl.BlockSpec(memory_space=pltpu.HBM)
    return pl.pallas_call(
        read_kernel,
        in_specs=[near, far, far, far, far],
        out_shape=jax.ShapeDtypeStruct((tokens, columns), BF16),
        scratch_shapes=[
            pltpu.VMEM(query.shape, query.dtype),
            pltpu.VMEM(intra.shape, intra.dtype),
            pltpu.VMEM(gate.shape, gate.dtype),
            pltpu.VMEM((pieces, width, columns // pieces), BF16),
            pltpu.VMEM((tokens, width), BF16),
            pltpu.SemaphoreType.DMA((3 + pieces,)),
        ],
        compiler_params=params(VMEM_WIDE),
        cost_estimate=cost(4),
        name="read_out",
    )(back, query, intra, gate, weight)


def group_size(count, heads):
    return max(s for s in range(1, 9) if count % s == 0 and heads % s == 0)


def local(queries, keys, values, out_gate, log_decay, beta, norm_gain, out_weight, owner):
    tokens, heads = keys.shape[1], log_decay.shape[1]
    count = lax.axis_size("seq")
    me = lax.axis_index("seq")
    size = group_size(count, heads)
    groups = count // size
    own = heads // size
    carried = max(1, own * (keys.shape[2] // DK) // heads)
    members = [[g * size + i for i in range(size)] for g in range(groups)]

    def swap(x):
        return lax.all_to_all(x, "seq", 0, 0, axis_index_groups=members, tiled=True)

    def hop(x, source, target):
        return lax.ppermute(x, "seq", [(source * size + i, target * size + i) for i in range(size)])

    mine = lax.dynamic_slice_in_dim(owner[0], (me % size) * own, own) - (me // size) * size
    info = jnp.concatenate([(me // size)[None].astype(jnp.int32), mine])

    raw = swap(pack(keys, values, log_decay, beta, size))
    query, intra, gate = local_part(queries, keys, values, out_gate, log_decay, beta, norm_gain[None])
    raw, query, intra, gate = lax.optimization_barrier((raw, query, intra, gate))
    move, add, pair = group_maps(raw, own, carried)
    if groups == 2:
        got = lax.ppermute(pair, "seq", [(i, (i + size) % count) for i in range(count)])
        sent = spread_states(pair_spread_kernel, info, move, add, pair, got)
    else:
        start = jnp.zeros((own, DK, DV), F32)
        wide = pair.astype(F32)

        def leave(start):
            kept = jnp.einsum("hij,hjk->hik", wide[..., :DK], start, precision=HIGH)
            return kept + wide[..., DK:]

        for g in range(groups - 1):
            start = start + hop(leave(start).astype(BF16), g, g + 1).astype(F32)
        last = leave(start).astype(BF16)
        last = jnp.where(me // size == groups - 1, last, jnp.zeros_like(last))
        for g in range(groups - 1, 0, -1):
            last = last + hop(last, g, g - 1)
        sent = spread_states(spread_kernel, info, move, add, start, last)
    back = swap(sent)
    back = back.reshape(heads, DK, 2 * DV)
    decode_states = back[None, :, :, DV:].astype(F32)
    partial_value = read_out(query, intra, gate, back, out_weight)
    ranks = lax.axis_size("head")
    if ranks == 2:
        half = tokens // 2
        rank = lax.axis_index("head")
        keep = lax.dynamic_slice_in_dim(partial_value, rank * half, half)
        give = lax.dynamic_slice_in_dim(partial_value, (1 - rank) * half, half)
        got = lax.ppermute(give, "head", [(0, 1), (1, 0)])
        total = (keep.astype(F32) + got.astype(F32)).astype(BF16)
    else:
        total = lax.psum_scatter(partial_value, "head", scatter_dimension=0, tiled=True)
    return (total[:, None, :], decode_states)


def solution(mesh):
    placed = (
        P(None, "seq", "head"),
        P(None, "seq", "head"),
        P(None, "seq", "head"),
        P(None, "seq", "head"),
        P(None, "head", "seq"),
        P(None, "head", "seq"),
        P(),
        P("head", None),
        P(None, "head"),
    )
    return jax.shard_map(
        local,
        mesh=mesh,
        in_specs=placed,
        out_specs=(P(("seq", "head"), None, None), P("seq", "head", None, None)),
        check_vma=False,
    )
```

```python
import jax
import jax.numpy as jnp
from jax import lax
from jax.experimental import pallas as pl
from jax.experimental.pallas import tpu as pltpu
from jax.sharding import PartitionSpec as P

DK = 128
DV = 128
SMALL = 16
EXTRA = 16
HIGH = lax.Precision.HIGHEST
F32 = jnp.float32
BF16 = jnp.bfloat16
VMEM_LIMIT = 40 * 1024 * 1024
VMEM_MOST = 63 * 1024 * 1024
VMEM_WIDE = 50 * 1024 * 1024
VMEM_LEAST = 4 * 1024 * 1024

NN = (((1,), (0,)), ((), ()))
NT = (((1,), (1,)), ((), ()))
TN = (((0,), (0,)), ((), ()))


def dot(a, b, dims=NN, precision=None):
    return lax.dot_general(a, b, dims, precision=precision, preferred_element_type=F32)


def split(x):
    high = x.astype(BF16)
    return high, (x - high.astype(F32)).astype(BF16)


def dot3(a, b):
    return dot(a[0], b[0]) + (dot(a[0], b[1]) + dot(a[1], b[0]))


def row_col(size):
    return (
        lax.broadcasted_iota(jnp.int32, (size, size), 0),
        lax.broadcasted_iota(jnp.int32, (size, size), 1),
    )


def inverses(systems, d_scr, t_scr):
    count, tokens = len(systems), systems[0].shape[0]
    blocks = tokens // SMALL
    row, col = row_col(tokens)
    same_small = (row // SMALL) == (col // SMALL)
    pick = jnp.where((row % SMALL) == col, 1.0, 0.0).astype(BF16)
    lane = lax.broadcasted_iota(jnp.int32, (blocks, tokens), 1)
    first = lax.broadcasted_iota(jnp.int32, (blocks, tokens), 0) * SMALL
    unit = [jnp.where(lane == first + i, 1.0, 0.0) for i in range(SMALL)]
    for u in range(count):
        high, low = split(jnp.where(same_small, systems[u], 0.0))
        d_scr[u] = dot(high, pick) + dot(low, pick)
    for u in range(count):
        rows = list(unit)
        coef = [d_scr[u, pl.ds(i, blocks, stride=SMALL), :] for i in range(SMALL)]
        for j in range(SMALL - 1):
            for i in range(j + 1, SMALL):
                rows[i] = rows[i] - coef[i][:, j : j + 1] * rows[j]
        for i in range(SMALL):
            t_scr[u, pl.ds(i, blocks, stride=SMALL), :] = rows[i]
    found = [t_scr[u] for u in range(count)]
    size = SMALL
    while 2 * size < tokens:
        mask = jnp.logical_and((row // (2 * size)) == (col // (2 * size)), (row // size) != (col // size))
        parts = [split(t) for t in found]
        inner = [dot3(split(jnp.where(mask, systems[u], 0.0)), parts[u]) for u in range(count)]
        found = [found[u] - dot3(parts[u], split(inner[u])) for u in range(count)]
        size *= 2
    upper = [split(t[:size, :size]) for t in found]
    lower = [split(t[size:, size:]) for t in found]
    inner = [dot3(split(systems[u][size:, :size]), upper[u]) for u in range(count)]
    corner = [dot3(lower[u], split(inner[u])) for u in range(count)]
    return [
        jnp.concatenate(
            [found[u][:size], jnp.concatenate([-corner[u], found[u][size:, size:]], axis=1)], axis=0
        )
        for u in range(count)
    ]


def norms(key, eye):
    gram = dot(key, key, NT)
    on_diag = jnp.where(eye, gram, 0.0)
    return (
        gram,
        lax.rsqrt(jnp.sum(on_diag, axis=1, keepdims=True) + 1e-6),
        lax.rsqrt(jnp.sum(on_diag, axis=0, keepdims=True) + 1e-6),
    )


def pack_kernel(k_ref, v_ref, g_ref, b_ref, out_ref, g_scr, b_scr, e_scr, sems):
    size = out_ref.shape[0]
    tokens, heads = g_ref.shape[2], g_ref.shape[1]
    own = heads // size
    repeat = heads // (k_ref.shape[2] // DK)
    keys = max(1, own // repeat)
    copies = [
        pltpu.make_async_copy(g_ref, g_scr, sems.at[0]),
        pltpu.make_async_copy(b_ref, b_scr, sems.at[1]),
    ]
    for d in range(size):
        for i in range(keys):
            kh = d * own // repeat + i
            copies.append(
                pltpu.make_async_copy(
                    k_ref.at[0, :, kh * DK : (kh + 1) * DK],
                    out_ref.at[d, i * tokens : (i + 1) * tokens],
                    sems.at[len(copies)],
                )
            )
        for i in range(own):
            h = d * own + i
            copies.append(
                pltpu.make_async_copy(
                    v_ref.at[0, :, h * DV : (h + 1) * DV],
                    out_ref.at[d, (keys + i) * tokens : (keys + i + 1) * tokens],
                    sems.at[len(copies)],
                )
            )
    for copy in copies:
        copy.start()
    copies[0].wait()
    copies[1].wait()
    e_scr[...] = jnp.zeros_like(e_scr)
    for which, scr in ((0, g_scr), (1, b_scr)):
        rest = scr[0]
        for part in range(3):
            piece = rest.astype(BF16).astype(F32)
            rest = rest - piece
            for d in range(size):
                at = part * 2 * own + which * own
                e_scr[d, at : at + own] = piece[d * own : (d + 1) * own]
    for d in range(size):
        out_ref[d, (keys + own) * tokens :] = e_scr[d].astype(BF16)
    for copy in copies[2:]:
        copy.wait()


def local_kernel(
    q_ref, k_ref, v_ref, z_ref, g_ref, b_ref, gain_ref, query_ref, intra_ref, gate_ref, d_scr, t_scr
):
    tokens = k_ref.shape[1]
    heads = g_ref.shape[1]
    repeat = heads // (k_ref.shape[2] // DK)
    row, col = row_col(tokens)
    lower = row >= col
    eye = row == col
    gates = g_ref[0]
    betas = b_ref[0]
    tri = jnp.where(lower, 1.0, 0.0)
    cum_cols = dot(tri, gates, NT, HIGH)
    cum_rows = dot(gates, tri, NT, HIGH)
    beta_cols = dot(jnp.where(eye, 1.0, 0.0), betas, NT, HIGH)
    gain = gain_ref[0:1, :]
    key_side = [norms(k_ref[0, :, i * DK : (i + 1) * DK], eye) for i in range(heads // repeat)]
    systems = []
    for h in range(heads):
        gram, key_col, key_row = key_side[h // repeat]
        decay = jnp.exp(jnp.where(row > col, cum_cols[:, h : h + 1] - cum_rows[h : h + 1, :], -1e30))
        systems.append(decay * gram * (beta_cols[:, h : h + 1] * key_col) * key_row)
    found = inverses(systems, d_scr, t_scr)
    for h in range(heads):
        kh = h // repeat
        _, key_col, key_row = key_side[kh]
        key = k_ref[0, :, kh * DK : (kh + 1) * DK]
        if h % repeat == 0:
            query = q_ref[0, :, kh * DK : (kh + 1) * DK]
            queryf = query.astype(F32)
            query_col = lax.rsqrt(jnp.sum(queryf * queryf, axis=1, keepdims=True) + 1e-6) * DK**-0.5
            product = dot(query, key, NT) * query_col * key_row
        scaled = found[h] * betas[h : h + 1, :]
        update = dot(scaled.astype(BF16), v_ref[0, :, h * DV : (h + 1) * DV])
        erase = dot((scaled * (jnp.exp(cum_rows[h : h + 1, :]) * key_row)).astype(BF16), key)
        both = jnp.concatenate([erase, update], axis=1).astype(BF16)
        decay = jnp.exp(jnp.where(lower, cum_cols[:, h : h + 1] - cum_rows[h : h + 1, :], -1e30))
        mixed = dot((decay * product).astype(BF16), both)
        intra_ref[:, h * DV : (h + 1) * DV] = mixed[:, DK:]
        reach = jnp.exp(cum_cols[:, h : h + 1]) * query_col
        query_ref[:, h * DK : (h + 1) * DK] = (reach * queryf - mixed[:, :DK]).astype(BF16)
        z = z_ref[0, :, h * DV : (h + 1) * DV].astype(F32)
        gate_ref[:, h * DV : (h + 1) * DV] = gain * z / (1.0 + jnp.exp(-z))


def group_kernel(own, keys, x_ref, move_ref, add_ref, pair_ref, y_scr, d_scr, t_scr):
    shards = x_ref.shape[0]
    tokens = DK
    repeat = own // keys
    row, col = row_col(tokens)
    lower = row >= col
    eye = row == col
    base = (keys + own) * tokens
    take_row = lax.broadcasted_iota(jnp.int32, (8, EXTRA), 0)
    take_col = lax.broadcasted_iota(jnp.int32, (8, EXTRA), 1)
    take = jnp.where(
        jnp.logical_and(take_col % (2 * own) == take_row, take_col < 6 * own), 1.0, 0.0
    ).astype(BF16)
    plain = jnp.concatenate([dot(take, x_ref[j, base : base + EXTRA]) for j in range(shards)], axis=0)
    tri = jnp.where(lower, 1.0, 0.0)
    cum_cols = dot(tri, plain, NT, HIGH)
    cum_rows = dot(plain, tri, NT, HIGH)
    plain_cols = dot(jnp.where(eye, 1.0, 0.0), plain, NT, HIGH)

    @pl.when(pl.program_id(0) == 0)
    def _():
        for h in range(own):
            y_scr[h] = jnp.concatenate(
                [jnp.where(eye, 1.0, 0.0), jnp.zeros((tokens, DV), F32)], axis=1
            )

    units = [(j, h) for j in range(shards) for h in range(own)]
    key_side = {}
    for j in range(shards):
        for i in range(keys):
            key_side[j, i] = norms(x_ref[j, i * tokens : (i + 1) * tokens], eye)
    systems = []
    for j, h in units:
        gram, key_col, key_row = key_side[j, h // repeat]
        at = j * 8 + h
        decay = jnp.exp(jnp.where(row > col, cum_cols[:, at : at + 1] - cum_rows[at : at + 1, :], -1e30))
        systems.append(decay * gram * (plain_cols[:, at + own : at + own + 1] * key_col) * key_row)
    found = inverses(systems, d_scr, t_scr)
    moved = {}
    for u, (j, h) in enumerate(units):
        i = h // repeat
        _, key_col, key_row = key_side[j, i]
        at = j * 8 + h
        key = x_ref[j, i * tokens : (i + 1) * tokens]
        value = x_ref[j, (keys + h) * tokens : (keys + h + 1) * tokens]
        scaled = found[u] * plain[at + own : at + own + 1, :]
        high, low = split(scaled)
        update = dot(high, value) + dot(low, value)
        high, low = split(scaled * (jnp.exp(cum_rows[at : at + 1, :]) * key_row))
        erase = dot(high, key) + dot(low, key)
        last = cum_rows[at : at + 1, tokens - 1 :]
        weight = jnp.exp(last - cum_cols[:, at : at + 1]) * key_col
        high, low = split(jnp.concatenate([erase, update], axis=1) * weight)
        both = dot(key, high, TN) + dot(key, low, TN)
        moved[j, h] = (jnp.where(eye, jnp.exp(last), 0.0) - both[:, :DK], both[:, DK:])
    total = [y_scr[h] for h in range(own)]
    for j in range(shards):
        for h in range(own):
            move_ref[j, h] = total[h][:, :DK].astype(BF16)
            add_ref[j, h] = total[h][:, DK:]
            gone = dot3(split(moved[j, h][0]), split(total[h]))
            total[h] = jnp.concatenate([gone[:, :DK], gone[:, DK:] + moved[j, h][1]], axis=1)
    for h in range(own):
        y_scr[h] = total[h]
        pair_ref[h] = total[h].astype(BF16)


def spread(start, final, info_ref, move_ref, add_ref, out_ref):
    size, own = move_ref.shape[0], move_ref.shape[1]
    for h in range(own):
        at = start[h].astype(BF16)
        to = info_ref[1 + h]
        for j in range(size):
            entry = dot(move_ref[j, h], at) + add_ref[j, h]
            kept = jnp.where(to == j, final[h], jnp.zeros_like(final[h]))
            out_ref[j, h] = jnp.concatenate([entry, kept], axis=1).astype(BF16)


def pair_spread_kernel(info_ref, move_ref, add_ref, mine_ref, got_ref, out_ref):
    own = mine_ref.shape[0]
    late = info_ref[0] == 1
    start, final = [], []
    for h in range(own):
        mine, got = mine_ref[h], got_ref[h]
        first = jnp.where(late, got[:, DK:].astype(F32), mine[:, DK:].astype(F32))
        second = jnp.where(late, mine.astype(F32), got.astype(F32))
        final.append(dot(second[:, :DK].astype(BF16), first.astype(BF16)) + second[:, DK:])
        start.append(jnp.where(late, first, jnp.zeros_like(first)))
    spread(start, final, info_ref, move_ref, add_ref, out_ref)


def spread_kernel(info_ref, move_ref, add_ref, start_ref, final_ref, out_ref):
    own = start_ref.shape[0]
    start = [start_ref[h].astype(F32) for h in range(own)]
    final = [final_ref[h].astype(F32) for h in range(own)]
    spread(start, final, info_ref, move_ref, add_ref, out_ref)


def read_kernel(back_ref, query_ref, intra_ref, gate_ref, w_ref, out_ref, q_scr, i_scr, z_scr, w_scr, normed_scr, sems):
    heads = back_ref.shape[0]
    pieces, step = w_scr.shape[0], w_scr.shape[2]
    copies = [
        pltpu.make_async_copy(query_ref, q_scr, sems.at[0]),
        pltpu.make_async_copy(intra_ref, i_scr, sems.at[1]),
        pltpu.make_async_copy(gate_ref, z_scr, sems.at[2]),
    ] + [
        pltpu.make_async_copy(w_ref.at[:, c * step : (c + 1) * step], w_scr.at[c], sems.at[3 + c])
        for c in range(pieces)
    ]
    for copy in copies:
        copy.start()
    for copy in copies[:3]:
        copy.wait()
    for h in range(heads):
        cols = slice(h * DV, (h + 1) * DV)
        value = i_scr[:, cols] + dot(q_scr[:, cols], back_ref[h, :, :DV])
        scale = lax.rsqrt(jnp.mean(value * value, axis=1, keepdims=True) + 1e-6)
        normed_scr[:, cols] = (value * scale * z_scr[:, cols]).astype(BF16)
    for c in range(pieces):
        copies[3 + c].wait()
        out_ref[:, c * step : (c + 1) * step] = dot(normed_scr[...], w_scr[c]).astype(BF16)


def cost(micros):
    return pl.CostEstimate(flops=int(micros * 1.15e9), bytes_accessed=1 << 20, transcendentals=0)


def params(limit=VMEM_LIMIT):
    return pltpu.CompilerParams(vmem_limit_bytes=limit)


def pack(keys, values, log_decay, beta, size):
    tokens, heads, key_heads = keys.shape[1], log_decay.shape[1], keys.shape[2] // DK
    own = heads // size
    carried = max(1, own * key_heads // heads)
    rows = (carried + own) * tokens + EXTRA
    far = pl.BlockSpec(memory_space=pltpu.HBM)
    return pl.pallas_call(
        pack_kernel,
        in_specs=[far, far, far, far],
        out_shape=jax.ShapeDtypeStruct((size, rows, DK), BF16),
        scratch_shapes=[
            pltpu.VMEM(log_decay.shape, F32),
            pltpu.VMEM(beta.shape, F32),
            pltpu.VMEM((size, EXTRA, tokens), F32),
            pltpu.SemaphoreType.DMA((2 + size * (carried + own),)),
        ],
        compiler_params=params(VMEM_MOST),
        cost_estimate=cost(2),
        name="pack",
    )(keys, values, log_decay, beta)


def local_part(queries, keys, values, out_gate, log_decay, beta, gain):
    tokens, heads, key_heads = keys.shape[1], log_decay.shape[1], keys.shape[2] // DK
    step = min(8, heads)
    key_step = step * key_heads // heads
    wide = pl.BlockSpec((tokens, step * DV), lambda i: (0, i))
    narrow = pl.BlockSpec((1, tokens, key_step * DK), lambda i: (0, 0, i))
    broad = pl.BlockSpec((1, tokens, step * DV), lambda i: (0, 0, i))
    thin = pl.BlockSpec((1, step, tokens), lambda i: (0, i, 0))
    return pl.pallas_call(
        local_kernel,
        grid=(heads // step,),
        in_specs=[narrow, narrow, broad, broad, thin, thin, pl.BlockSpec((1, DV), lambda i: (0, 0))],
        out_specs=[wide, wide, wide],
        out_shape=[
            jax.ShapeDtypeStruct((tokens, heads * DK), BF16),
            jax.ShapeDtypeStruct((tokens, heads * DV), F32),
            jax.ShapeDtypeStruct((tokens, heads * DV), F32),
        ],
        scratch_shapes=[pltpu.VMEM((step, tokens, DK), F32), pltpu.VMEM((step, tokens, tokens), F32)],
        compiler_params=params(VMEM_MOST),
        cost_estimate=cost(12),
        name="local_part",
    )(queries, keys, values, out_gate, log_decay, beta, gain)


def group_maps(x, own, keys):
    size, rows = x.shape[0], x.shape[1]
    step = size
    block = lambda i: (i, 0, 0, 0)
    return pl.pallas_call(
        lambda *refs: group_kernel(own, keys, *refs),
        grid=(size // step,),
        in_specs=[pl.BlockSpec((step, rows, DK), lambda i: (i, 0, 0))],
        out_specs=[
            pl.BlockSpec((step, own, DK, DK), block),
            pl.BlockSpec((step, own, DK, DV), block),
            pl.BlockSpec((own, DK, DK + DV), lambda i: (0, 0, 0)),
        ],
        out_shape=[
            jax.ShapeDtypeStruct((size, own, DK, DK), BF16),
            jax.ShapeDtypeStruct((size, own, DK, DV), F32),
            jax.ShapeDtypeStruct((own, DK, DK + DV), BF16),
        ],
        scratch_shapes=[
            pltpu.VMEM((own, DK, DK + DV), F32),
            pltpu.VMEM((step * own, DK, DK), F32),
            pltpu.VMEM((step * own, DK, DK), F32),
        ],
        compiler_params=params(),
        cost_estimate=cost(12),
        name="group_maps",
    )(x)


def spread_states(kernel, info, move, add, one, two):
    near = pl.BlockSpec(memory_space=pltpu.VMEM)
    size, own = move.shape[0], move.shape[1]
    return pl.pallas_call(
        kernel,
        in_specs=[pl.BlockSpec(memory_space=pltpu.SMEM), near, near, near, near],
        out_shape=jax.ShapeDtypeStruct((size, own, DK, 2 * DV), BF16),
        compiler_params=params(),
        cost_estimate=cost(2),
        name="spread_states",
    )(info, move, add, one, two)


def read_out(query, intra, gate, back, weight):
    tokens, width = query.shape
    columns = weight.shape[1]
    pieces = 8
    near = pl.BlockSpec(memory_space=pltpu.VMEM)
    far = pl.BlockSpec(memory_space=pltpu.HBM)
    return pl.pallas_call(
        read_kernel,
        in_specs=[near, far, far, far, far],
        out_shape=jax.ShapeDtypeStruct((tokens, columns), BF16),
        scratch_shapes=[
            pltpu.VMEM(query.shape, query.dtype),
            pltpu.VMEM(intra.shape, intra.dtype),
            pltpu.VMEM(gate.shape, gate.dtype),
            pltpu.VMEM((pieces, width, columns // pieces), BF16),
            pltpu.VMEM((tokens, width), BF16),
            pltpu.SemaphoreType.DMA((3 + pieces,)),
        ],
        compiler_params=params(VMEM_WIDE),
        cost_estimate=cost(4),
        name="read_out",
    )(back, query, intra, gate, weight)


def group_size(count, heads):
    return max(s for s in range(1, 9) if count % s == 0 and heads % s == 0)


def local(queries, keys, values, out_gate, log_decay, beta, norm_gain, out_weight, owner):
    tokens, heads = keys.shape[1], log_decay.shape[1]
    count = lax.axis_size("seq")
    me = lax.axis_index("seq")
    size = group_size(count, heads)
    groups = count // size
    own = heads // size
    carried = max(1, own * (keys.shape[2] // DK) // heads)
    members = [[g * size + i for i in range(size)] for g in range(groups)]

    def swap(x):
        return lax.all_to_all(x, "seq", 0, 0, axis_index_groups=members, tiled=True)

    def hop(x, source, target):
        return lax.ppermute(x, "seq", [(source * size + i, target * size + i) for i in range(size)])

    mine = lax.dynamic_slice_in_dim(owner[0], (me % size) * own, own) - (me // size) * size
    info = jnp.concatenate([(me // size)[None].astype(jnp.int32), mine])

    raw = swap(pack(keys, values, log_decay, beta, size))
    query, intra, gate = local_part(queries, keys, values, out_gate, log_decay, beta, norm_gain[None])
    raw, query, intra, gate = lax.optimization_barrier((raw, query, intra, gate))
    move, add, pair = group_maps(raw, own, carried)
    if groups == 2:
        got = lax.ppermute(pair, "seq", [(i, (i + size) % count) for i in range(count)])
        sent = spread_states(pair_spread_kernel, info, move, add, pair, got)
    else:
        start = jnp.zeros((own, DK, DV), F32)
        wide = pair.astype(F32)

        def leave(start):
            kept = jnp.einsum("hij,hjk->hik", wide[..., :DK], start, precision=HIGH)
            return kept + wide[..., DK:]

        for g in range(groups - 1):
            start = start + hop(leave(start).astype(BF16), g, g + 1).astype(F32)
        last = leave(start).astype(BF16)
        last = jnp.where(me // size == groups - 1, last, jnp.zeros_like(last))
        for g in range(groups - 1, 0, -1):
            last = last + hop(last, g, g - 1)
        sent = spread_states(spread_kernel, info, move, add, start, last)
    back = swap(sent)
    back = back.reshape(heads, DK, 2 * DV)
    decode_states = back[None, :, :, DV:].astype(F32)
    partial_value = read_out(query, intra, gate, back, out_weight)
    ranks = lax.axis_size("head")
    if ranks == 2:
        half = tokens // 2
        rank = lax.axis_index("head")
        keep = lax.dynamic_slice_in_dim(partial_value, rank * half, half)
        give = lax.dynamic_slice_in_dim(partial_value, (1 - rank) * half, half)
        got = lax.ppermute(give, "head", [(0, 1), (1, 0)])
        total = (keep.astype(F32) + got.astype(F32)).astype(BF16)
    else:
        total = lax.psum_scatter(partial_value, "head", scatter_dimension=0, tiled=True)
    return (total[:, None, :], decode_states)


def solution(mesh):
    placed = (
        P(None, "seq", "head"),
        P(None, "seq", "head"),
        P(None, "seq", "head"),
        P(None, "seq", "head"),
        P(None, "head", "seq"),
        P(None, "head", "seq"),
        P(),
        P("head", None),
        P(None, "head"),
    )
    return jax.shard_map(
        local,
        mesh=mesh,
        in_specs=placed,
        out_specs=(P(("seq", "head"), None, None), P("seq", "head", None, None)),
        check_vma=False,
    )
```

```python
import jax
import jax.numpy as jnp
from jax import lax
from jax.experimental import pallas as pl
from jax.experimental.pallas import tpu as pltpu
from jax.sharding import PartitionSpec as P

DK = 128
DV = 128
SMALL = 16
EXTRA = 16
HIGH = lax.Precision.HIGHEST
F32 = jnp.float32
BF16 = jnp.bfloat16
VMEM_LIMIT = 40 * 1024 * 1024
VMEM_MOST = 63 * 1024 * 1024
VMEM_WIDE = 50 * 1024 * 1024
VMEM_LEAST = 4 * 1024 * 1024

NN = (((1,), (0,)), ((), ()))
NT = (((1,), (1,)), ((), ()))
TN = (((0,), (0,)), ((), ()))


def dot(a, b, dims=NN, precision=None):
    return lax.dot_general(a, b, dims, precision=precision, preferred_element_type=F32)


def split(x):
    high = x.astype(BF16)
    return high, (x - high.astype(F32)).astype(BF16)


def dot3(a, b):
    return dot(a[0], b[0]) + (dot(a[0], b[1]) + dot(a[1], b[0]))


def row_col(size):
    return (
        lax.broadcasted_iota(jnp.int32, (size, size), 0),
        lax.broadcasted_iota(jnp.int32, (size, size), 1),
    )


def inverses(systems, d_scr, t_scr):
    count, tokens = len(systems), systems[0].shape[0]
    blocks = tokens // SMALL
    row, col = row_col(tokens)
    same_small = (row // SMALL) == (col // SMALL)
    pick = jnp.where((row % SMALL) == col, 1.0, 0.0).astype(BF16)
    lane = lax.broadcasted_iota(jnp.int32, (blocks, tokens), 1)
    first = lax.broadcasted_iota(jnp.int32, (blocks, tokens), 0) * SMALL
    unit = [jnp.where(lane == first + i, 1.0, 0.0) for i in range(SMALL)]
    for u in range(count):
        high, low = split(jnp.where(same_small, systems[u], 0.0))
        d_scr[u] = dot(high, pick) + dot(low, pick)
    for u in range(count):
        rows = list(unit)
        coef = [d_scr[u, pl.ds(i, blocks, stride=SMALL), :] for i in range(SMALL)]
        for j in range(SMALL - 1):
            for i in range(j + 1, SMALL):
                rows[i] = rows[i] - coef[i][:, j : j + 1] * rows[j]
        for i in range(SMALL):
            t_scr[u, pl.ds(i, blocks, stride=SMALL), :] = rows[i]
    found = [t_scr[u] for u in range(count)]
    size = SMALL
    while 2 * size < tokens:
        mask = jnp.logical_and((row // (2 * size)) == (col // (2 * size)), (row // size) != (col // size))
        parts = [split(t) for t in found]
        inner = [dot3(split(jnp.where(mask, systems[u], 0.0)), parts[u]) for u in range(count)]
        found = [found[u] - dot3(parts[u], split(inner[u])) for u in range(count)]
        size *= 2
    upper = [split(t[:size, :size]) for t in found]
    lower = [split(t[size:, size:]) for t in found]
    inner = [dot3(split(systems[u][size:, :size]), upper[u]) for u in range(count)]
    corner = [dot3(lower[u], split(inner[u])) for u in range(count)]
    return [
        jnp.concatenate(
            [found[u][:size], jnp.concatenate([-corner[u], found[u][size:, size:]], axis=1)], axis=0
        )
        for u in range(count)
    ]


def norms(key, eye):
    gram = dot(key, key, NT)
    on_diag = jnp.where(eye, gram, 0.0)
    return (
        gram,
        lax.rsqrt(jnp.sum(on_diag, axis=1, keepdims=True) + 1e-6),
        lax.rsqrt(jnp.sum(on_diag, axis=0, keepdims=True) + 1e-6),
    )


def pack_kernel(k_ref, v_ref, g_ref, b_ref, out_ref, g_scr, b_scr, e_scr, sems):
    size = out_ref.shape[0]
    tokens, heads = g_ref.shape[2], g_ref.shape[1]
    own = heads // size
    repeat = heads // (k_ref.shape[2] // DK)
    keys = max(1, own // repeat)
    copies = [
        pltpu.make_async_copy(g_ref, g_scr, sems.at[0]),
        pltpu.make_async_copy(b_ref, b_scr, sems.at[1]),
    ]
    for d in range(size):
        for i in range(keys):
            kh = d * own // repeat + i
            copies.append(
                pltpu.make_async_copy(
                    k_ref.at[0, :, kh * DK : (kh + 1) * DK],
                    out_ref.at[d, i * tokens : (i + 1) * tokens],
                    sems.at[len(copies)],
                )
            )
        for i in range(own):
            h = d * own + i
            copies.append(
                pltpu.make_async_copy(
                    v_ref.at[0, :, h * DV : (h + 1) * DV],
                    out_ref.at[d, (keys + i) * tokens : (keys + i + 1) * tokens],
                    sems.at[len(copies)],
                )
            )
    for copy in copies:
        copy.start()
    copies[0].wait()
    copies[1].wait()
    e_scr[...] = jnp.zeros_like(e_scr)
    for which, scr in ((0, g_scr), (1, b_scr)):
        rest = scr[0]
        for part in range(3):
            piece = rest.astype(BF16).astype(F32)
            rest = rest - piece
            for d in range(size):
                at = part * 2 * own + which * own
                e_scr[d, at : at + own] = piece[d * own : (d + 1) * own]
    for d in range(size):
        out_ref[d, (keys + own) * tokens :] = e_scr[d].astype(BF16)
    for copy in copies[2:]:
        copy.wait()


def local_kernel(
    q_ref, k_ref, v_ref, z_ref, g_ref, b_ref, gain_ref, query_ref, intra_ref, gate_ref, d_scr, t_scr
):
    tokens = k_ref.shape[1]
    heads = g_ref.shape[1]
    repeat = heads // (k_ref.shape[2] // DK)
    row, col = row_col(tokens)
    lower = row >= col
    eye = row == col
    gates = g_ref[0]
    betas = b_ref[0]
    tri = jnp.where(lower, 1.0, 0.0)
    cum_cols = dot(tri, gates, NT, HIGH)
    cum_rows = dot(gates, tri, NT, HIGH)
    beta_cols = dot(jnp.where(eye, 1.0, 0.0), betas, NT, HIGH)
    gain = gain_ref[0:1, :]
    key_side = [norms(k_ref[0, :, i * DK : (i + 1) * DK], eye) for i in range(heads // repeat)]
    systems = []
    for h in range(heads):
        gram, key_col, key_row = key_side[h // repeat]
        decay = jnp.exp(jnp.where(row > col, cum_cols[:, h : h + 1] - cum_rows[h : h + 1, :], -1e30))
        systems.append(decay * gram * (beta_cols[:, h : h + 1] * key_col) * key_row)
    found = inverses(systems, d_scr, t_scr)
    for h in range(heads):
        kh = h // repeat
        _, key_col, key_row = key_side[kh]
        key = k_ref[0, :, kh * DK : (kh + 1) * DK]
        if h % repeat == 0:
            query = q_ref[0, :, kh * DK : (kh + 1) * DK]
            queryf = query.astype(F32)
            query_col = lax.rsqrt(jnp.sum(queryf * queryf, axis=1, keepdims=True) + 1e-6) * DK**-0.5
            product = dot(query, key, NT) * query_col * key_row
        scaled = found[h] * betas[h : h + 1, :]
        update = dot(scaled.astype(BF16), v_ref[0, :, h * DV : (h + 1) * DV])
        erase = dot((scaled * (jnp.exp(cum_rows[h : h + 1, :]) * key_row)).astype(BF16), key)
        both = jnp.concatenate([erase, update], axis=1).astype(BF16)
        decay = jnp.exp(jnp.where(lower, cum_cols[:, h : h + 1] - cum_rows[h : h + 1, :], -1e30))
        mixed = dot((decay * product).astype(BF16), both)
        intra_ref[:, h * DV : (h + 1) * DV] = mixed[:, DK:]
        reach = jnp.exp(cum_cols[:, h : h + 1]) * query_col
        query_ref[:, h * DK : (h + 1) * DK] = (reach * queryf - mixed[:, :DK]).astype(BF16)
        z = z_ref[0, :, h * DV : (h + 1) * DV].astype(F32)
        gate_ref[:, h * DV : (h + 1) * DV] = gain * z / (1.0 + jnp.exp(-z))


def group_kernel(own, keys, x_ref, move_ref, add_ref, pair_ref, d_scr, t_scr):
    shards = x_ref.shape[0]
    tokens = DK
    repeat = own // keys
    row, col = row_col(tokens)
    lower = row >= col
    eye = row == col
    base = (keys + own) * tokens
    take_row = lax.broadcasted_iota(jnp.int32, (8, EXTRA), 0)
    take_col = lax.broadcasted_iota(jnp.int32, (8, EXTRA), 1)
    take = jnp.where(
        jnp.logical_and(take_col % (2 * own) == take_row, take_col < 6 * own), 1.0, 0.0
    ).astype(BF16)
    plain = jnp.concatenate([dot(take, x_ref[j, base : base + EXTRA]) for j in range(shards)], axis=0)
    tri = jnp.where(lower, 1.0, 0.0)
    cum_cols = dot(tri, plain, NT, HIGH)
    cum_rows = dot(plain, tri, NT, HIGH)
    plain_cols = dot(jnp.where(eye, 1.0, 0.0), plain, NT, HIGH)

    units = [(j, h) for j in range(shards) for h in range(own)]
    key_side = {}
    for j in range(shards):
        for i in range(keys):
            key_side[j, i] = norms(x_ref[j, i * tokens : (i + 1) * tokens], eye)
    systems = []
    for j, h in units:
        gram, key_col, key_row = key_side[j, h // repeat]
        at = j * 8 + h
        decay = jnp.exp(jnp.where(row > col, cum_cols[:, at : at + 1] - cum_rows[at : at + 1, :], -1e30))
        systems.append(decay * gram * (plain_cols[:, at + own : at + own + 1] * key_col) * key_row)
    found = inverses(systems, d_scr, t_scr)
    rows_at = [j * 8 + h for j, h in units]
    keys_of = [x_ref[j, (h // repeat) * tokens : (h // repeat + 1) * tokens] for j, h in units]
    values_of = [x_ref[j, (keys + h) * tokens : (keys + h + 1) * tokens] for j, h in units]
    sides = [key_side[j, h // repeat] for j, h in units]
    count = range(len(units))
    scaled = [found[u] * plain[rows_at[u] + own : rows_at[u] + own + 1, :] for u in count]
    forward = [jnp.exp(cum_rows[at : at + 1, :]) * side[2] for at, side in zip(rows_at, sides)]
    left = [split(scaled[u]) for u in count]
    right = [split(scaled[u] * forward[u]) for u in count]
    update = [dot(left[u][0], values_of[u]) + dot(left[u][1], values_of[u]) for u in count]
    erase = [dot(right[u][0], keys_of[u]) + dot(right[u][1], keys_of[u]) for u in count]
    lasts = [cum_rows[at : at + 1, tokens - 1 :] for at in rows_at]
    weights = [
        jnp.exp(lasts[u] - cum_cols[:, rows_at[u] : rows_at[u] + 1]) * sides[u][1] for u in count
    ]
    solved = [split(jnp.concatenate([erase[u], update[u]], axis=1) * weights[u]) for u in count]
    both = [dot(keys_of[u], solved[u][0], TN) + dot(keys_of[u], solved[u][1], TN) for u in count]
    moved = {
        units[u]: (jnp.where(eye, jnp.exp(lasts[u]), 0.0) - both[u][:, :DK], both[u][:, DK:])
        for u in count
    }
    start = jnp.concatenate([jnp.where(eye, 1.0, 0.0), jnp.zeros((tokens, DV), F32)], axis=1)
    total = [start for _ in range(own)]
    for j in range(shards):
        for h in range(own):
            move_ref[j, h] = total[h][:, :DK].astype(BF16)
            add_ref[j, h] = total[h][:, DK:]
            gone = dot3(split(moved[j, h][0]), split(total[h]))
            total[h] = jnp.concatenate([gone[:, :DK], gone[:, DK:] + moved[j, h][1]], axis=1)
    for h in range(own):
        pair_ref[h] = total[h].astype(BF16)


def spread(start, final, info_ref, move_ref, add_ref, out_ref):
    size, own = move_ref.shape[0], move_ref.shape[1]
    for h in range(own):
        at = start[h].astype(BF16)
        to = info_ref[1 + h]
        for j in range(size):
            entry = dot(move_ref[j, h], at) + add_ref[j, h]
            kept = jnp.where(to == j, final[h], jnp.zeros_like(final[h]))
            out_ref[j, h] = jnp.concatenate([entry, kept], axis=1).astype(BF16)


def pair_spread_kernel(info_ref, move_ref, add_ref, mine_ref, got_ref, out_ref):
    own = mine_ref.shape[0]
    late = info_ref[0] == 1
    start, final = [], []
    for h in range(own):
        mine, got = mine_ref[h], got_ref[h]
        first = jnp.where(late, got[:, DK:].astype(F32), mine[:, DK:].astype(F32))
        second = jnp.where(late, mine.astype(F32), got.astype(F32))
        final.append(dot(second[:, :DK].astype(BF16), first.astype(BF16)) + second[:, DK:])
        start.append(jnp.where(late, first, jnp.zeros_like(first)))
    spread(start, final, info_ref, move_ref, add_ref, out_ref)


def spread_kernel(info_ref, move_ref, add_ref, start_ref, final_ref, out_ref):
    own = start_ref.shape[0]
    start = [start_ref[h].astype(F32) for h in range(own)]
    final = [final_ref[h].astype(F32) for h in range(own)]
    spread(start, final, info_ref, move_ref, add_ref, out_ref)


def read_kernel(back_ref, query_ref, intra_ref, gate_ref, w_ref, out_ref, q_scr, i_scr, z_scr, w_scr, normed_scr, sems):
    heads = back_ref.shape[0]
    pieces, step = w_scr.shape[0], w_scr.shape[2]
    copies = [
        pltpu.make_async_copy(query_ref, q_scr, sems.at[0]),
        pltpu.make_async_copy(intra_ref, i_scr, sems.at[1]),
        pltpu.make_async_copy(gate_ref, z_scr, sems.at[2]),
    ] + [
        pltpu.make_async_copy(w_ref.at[:, c * step : (c + 1) * step], w_scr.at[c], sems.at[3 + c])
        for c in range(pieces)
    ]
    for copy in copies:
        copy.start()
    for copy in copies[:3]:
        copy.wait()
    for h in range(heads):
        cols = slice(h * DV, (h + 1) * DV)
        value = i_scr[:, cols] + dot(q_scr[:, cols], back_ref[h, :, :DV])
        scale = lax.rsqrt(jnp.mean(value * value, axis=1, keepdims=True) + 1e-6)
        normed_scr[:, cols] = (value * scale * z_scr[:, cols]).astype(BF16)
    for c in range(pieces):
        copies[3 + c].wait()
        out_ref[:, c * step : (c + 1) * step] = dot(normed_scr[...], w_scr[c]).astype(BF16)


def cost(micros):
    return pl.CostEstimate(flops=int(micros * 1.15e9), bytes_accessed=1 << 20, transcendentals=0)


def params(limit=VMEM_LIMIT):
    return pltpu.CompilerParams(vmem_limit_bytes=limit)


def pack(keys, values, log_decay, beta, size):
    tokens, heads, key_heads = keys.shape[1], log_decay.shape[1], keys.shape[2] // DK
    own = heads // size
    carried = max(1, own * key_heads // heads)
    rows = (carried + own) * tokens + EXTRA
    far = pl.BlockSpec(memory_space=pltpu.HBM)
    return pl.pallas_call(
        pack_kernel,
        in_specs=[far, far, far, far],
        out_shape=jax.ShapeDtypeStruct((size, rows, DK), BF16),
        scratch_shapes=[
            pltpu.VMEM(log_decay.shape, F32),
            pltpu.VMEM(beta.shape, F32),
            pltpu.VMEM((size, EXTRA, tokens), F32),
            pltpu.SemaphoreType.DMA((2 + size * (carried + own),)),
        ],
        compiler_params=params(VMEM_MOST),
        cost_estimate=cost(2),
        name="pack",
    )(keys, values, log_decay, beta)


def local_part(queries, keys, values, out_gate, log_decay, beta, gain):
    tokens, heads, key_heads = keys.shape[1], log_decay.shape[1], keys.shape[2] // DK
    step = min(8, heads)
    key_step = step * key_heads // heads
    wide = pl.BlockSpec((tokens, step * DV), lambda i: (0, i))
    narrow = pl.BlockSpec((1, tokens, key_step * DK), lambda i: (0, 0, i))
    broad = pl.BlockSpec((1, tokens, step * DV), lambda i: (0, 0, i))
    thin = pl.BlockSpec((1, step, tokens), lambda i: (0, i, 0))
    return pl.pallas_call(
        local_kernel,
        grid=(heads // step,),
        in_specs=[narrow, narrow, broad, broad, thin, thin, pl.BlockSpec((1, DV), lambda i: (0, 0))],
        out_specs=[wide, wide, wide],
        out_shape=[
            jax.ShapeDtypeStruct((tokens, heads * DK), BF16),
            jax.ShapeDtypeStruct((tokens, heads * DV), F32),
            jax.ShapeDtypeStruct((tokens, heads * DV), F32),
        ],
        scratch_shapes=[pltpu.VMEM((step, tokens, DK), F32), pltpu.VMEM((step, tokens, tokens), F32)],
        compiler_params=params(VMEM_MOST),
        cost_estimate=cost(12),
        name="local_part",
    )(queries, keys, values, out_gate, log_decay, beta, gain)


def group_maps(x, own, keys):
    size = x.shape[0]
    near = pl.BlockSpec(memory_space=pltpu.VMEM)
    return pl.pallas_call(
        lambda *refs: group_kernel(own, keys, *refs),
        in_specs=[near],
        out_specs=[near, near, near],
        out_shape=[
            jax.ShapeDtypeStruct((size, own, DK, DK), BF16),
            jax.ShapeDtypeStruct((size, own, DK, DV), F32),
            jax.ShapeDtypeStruct((own, DK, DK + DV), BF16),
        ],
        scratch_shapes=[
            pltpu.VMEM((size * own, DK, DK), F32),
            pltpu.VMEM((size * own, DK, DK), F32),
        ],
        compiler_params=params(),
        cost_estimate=cost(12),
        name="group_maps",
    )(x)


def spread_states(kernel, info, move, add, one, two):
    near = pl.BlockSpec(memory_space=pltpu.VMEM)
    size, own = move.shape[0], move.shape[1]
    return pl.pallas_call(
        kernel,
        in_specs=[pl.BlockSpec(memory_space=pltpu.SMEM), near, near, near, near],
        out_shape=jax.ShapeDtypeStruct((size, own, DK, 2 * DV), BF16),
        compiler_params=params(),
        cost_estimate=cost(2),
        name="spread_states",
    )(info, move, add, one, two)


def read_out(query, intra, gate, back, weight):
    tokens, width = query.shape
    columns = weight.shape[1]
    pieces = 8
    near = pl.BlockSpec(memory_space=pltpu.VMEM)
    far = pl.BlockSpec(memory_space=pltpu.HBM)
    return pl.pallas_call(
        read_kernel,
        in_specs=[near, far, far, far, far],
        out_shape=jax.ShapeDtypeStruct((tokens, columns), BF16),
        scratch_shapes=[
            pltpu.VMEM(query.shape, query.dtype),
            pltpu.VMEM(intra.shape, intra.dtype),
            pltpu.VMEM(gate.shape, gate.dtype),
            pltpu.VMEM((pieces, width, columns // pieces), BF16),
            pltpu.VMEM((tokens, width), BF16),
            pltpu.SemaphoreType.DMA((3 + pieces,)),
        ],
        compiler_params=params(VMEM_WIDE),
        cost_estimate=cost(4),
        name="read_out",
    )(back, query, intra, gate, weight)


def group_size(count, heads):
    return max(s for s in range(1, 9) if count % s == 0 and heads % s == 0)


def local(queries, keys, values, out_gate, log_decay, beta, norm_gain, out_weight, owner):
    tokens, heads = keys.shape[1], log_decay.shape[1]
    count = lax.axis_size("seq")
    me = lax.axis_index("seq")
    size = group_size(count, heads)
    groups = count // size
    own = heads // size
    carried = max(1, own * (keys.shape[2] // DK) // heads)
    members = [[g * size + i for i in range(size)] for g in range(groups)]

    def swap(x):
        return lax.all_to_all(x, "seq", 0, 0, axis_index_groups=members, tiled=True)

    def hop(x, source, target):
        return lax.ppermute(x, "seq", [(source * size + i, target * size + i) for i in range(size)])

    mine = lax.dynamic_slice_in_dim(owner[0], (me % size) * own, own) - (me // size) * size
    info = jnp.concatenate([(me // size)[None].astype(jnp.int32), mine])

    raw = swap(pack(keys, values, log_decay, beta, size))
    query, intra, gate = local_part(queries, keys, values, out_gate, log_decay, beta, norm_gain[None])
    raw, query, intra, gate = lax.optimization_barrier((raw, query, intra, gate))
    move, add, pair = group_maps(raw, own, carried)
    if groups == 2:
        got = lax.ppermute(pair, "seq", [(i, (i + size) % count) for i in range(count)])
        sent = spread_states(pair_spread_kernel, info, move, add, pair, got)
    else:
        start = jnp.zeros((own, DK, DV), F32)
        wide = pair.astype(F32)

        def leave(start):
            kept = jnp.einsum("hij,hjk->hik", wide[..., :DK], start, precision=HIGH)
            return kept + wide[..., DK:]

        for g in range(groups - 1):
            start = start + hop(leave(start).astype(BF16), g, g + 1).astype(F32)
        last = leave(start).astype(BF16)
        last = jnp.where(me // size == groups - 1, last, jnp.zeros_like(last))
        for g in range(groups - 1, 0, -1):
            last = last + hop(last, g, g - 1)
        sent = spread_states(spread_kernel, info, move, add, start, last)
    back = swap(sent)
    back = back.reshape(heads, DK, 2 * DV)
    decode_states = back[None, :, :, DV:].astype(F32)
    partial_value = read_out(query, intra, gate, back, out_weight)
    ranks = lax.axis_size("head")
    if ranks == 2:
        half = tokens // 2
        rank = lax.axis_index("head")
        keep = lax.dynamic_slice_in_dim(partial_value, rank * half, half)
        give = lax.dynamic_slice_in_dim(partial_value, (1 - rank) * half, half)
        got = lax.ppermute(give, "head", [(0, 1), (1, 0)])
        total = (keep.astype(F32) + got.astype(F32)).astype(BF16)
    else:
        total = lax.psum_scatter(partial_value, "head", scatter_dimension=0, tiled=True)
    return (total[:, None, :], decode_states)


def solution(mesh):
    placed = (
        P(None, "seq", "head"),
        P(None, "seq", "head"),
        P(None, "seq", "head"),
        P(None, "seq", "head"),
        P(None, "head", "seq"),
        P(None, "head", "seq"),
        P(),
        P("head", None),
        P(None, "head"),
    )
    return jax.shard_map(
        local,
        mesh=mesh,
        in_specs=placed,
        out_specs=(P(("seq", "head"), None, None), P("seq", "head", None, None)),
        check_vma=False,
    )
```

```python
import jax
import jax.numpy as jnp
from jax import lax
from jax.experimental import pallas as pl
from jax.experimental.pallas import tpu as pltpu
from jax.sharding import PartitionSpec as P

DK = 128
DV = 128
SMALL = 16
EXTRA = 16
HIGH = lax.Precision.HIGHEST
F32 = jnp.float32
BF16 = jnp.bfloat16
VMEM_LIMIT = 40 * 1024 * 1024
VMEM_MOST = 63 * 1024 * 1024
VMEM_WIDE = 50 * 1024 * 1024
VMEM_LEAST = 4 * 1024 * 1024

NN = (((1,), (0,)), ((), ()))
NT = (((1,), (1,)), ((), ()))
TN = (((0,), (0,)), ((), ()))


def dot(a, b, dims=NN, precision=None):
    return lax.dot_general(a, b, dims, precision=precision, preferred_element_type=F32)


def split(x):
    high = x.astype(BF16)
    return high, (x - high.astype(F32)).astype(BF16)


def dot3(a, b):
    return dot(a[0], b[0]) + (dot(a[0], b[1]) + dot(a[1], b[0]))


def row_col(size):
    return (
        lax.broadcasted_iota(jnp.int32, (size, size), 0),
        lax.broadcasted_iota(jnp.int32, (size, size), 1),
    )


def inverses(systems, d_scr, t_scr):
    count, tokens = len(systems), systems[0].shape[0]
    blocks = tokens // SMALL
    row, col = row_col(tokens)
    same_small = (row // SMALL) == (col // SMALL)
    pick = jnp.where((row % SMALL) == col, 1.0, 0.0).astype(BF16)
    lane = lax.broadcasted_iota(jnp.int32, (blocks, tokens), 1)
    first = lax.broadcasted_iota(jnp.int32, (blocks, tokens), 0) * SMALL
    unit = [jnp.where(lane == first + i, 1.0, 0.0) for i in range(SMALL)]
    for u in range(count):
        high, low = split(jnp.where(same_small, systems[u], 0.0))
        d_scr[u] = dot(high, pick) + dot(low, pick)
    for u in range(count):
        rows = list(unit)
        coef = [d_scr[u, pl.ds(i, blocks, stride=SMALL), :] for i in range(SMALL)]
        for j in range(SMALL - 1):
            for i in range(j + 1, SMALL):
                rows[i] = rows[i] - coef[i][:, j : j + 1] * rows[j]
        for i in range(SMALL):
            t_scr[u, pl.ds(i, blocks, stride=SMALL), :] = rows[i]
    found = [t_scr[u] for u in range(count)]
    size = SMALL
    while 2 * size < tokens:
        mask = jnp.logical_and((row // (2 * size)) == (col // (2 * size)), (row // size) != (col // size))
        parts = [split(t) for t in found]
        inner = [dot3(split(jnp.where(mask, systems[u], 0.0)), parts[u]) for u in range(count)]
        found = [found[u] - dot3(parts[u], split(inner[u])) for u in range(count)]
        size *= 2
    upper = [split(t[:size, :size]) for t in found]
    lower = [split(t[size:, size:]) for t in found]
    inner = [dot3(split(systems[u][size:, :size]), upper[u]) for u in range(count)]
    corner = [dot3(lower[u], split(inner[u])) for u in range(count)]
    return [
        jnp.concatenate(
            [found[u][:size], jnp.concatenate([-corner[u], found[u][size:, size:]], axis=1)], axis=0
        )
        for u in range(count)
    ]


def norms(key, eye):
    gram = dot(key, key, NT)
    on_diag = jnp.where(eye, gram, 0.0)
    return (
        gram,
        lax.rsqrt(jnp.sum(on_diag, axis=1, keepdims=True) + 1e-6),
        lax.rsqrt(jnp.sum(on_diag, axis=0, keepdims=True) + 1e-6),
    )


def pack_kernel(k_ref, v_ref, g_ref, b_ref, out_ref, g_scr, b_scr, e_scr, sems):
    size = out_ref.shape[0]
    tokens, heads = g_ref.shape[2], g_ref.shape[1]
    own = heads // size
    repeat = heads // (k_ref.shape[2] // DK)
    keys = max(1, own // repeat)
    copies = [
        pltpu.make_async_copy(g_ref, g_scr, sems.at[0]),
        pltpu.make_async_copy(b_ref, b_scr, sems.at[1]),
    ]
    for d in range(size):
        for i in range(keys):
            kh = d * own // repeat + i
            copies.append(
                pltpu.make_async_copy(
                    k_ref.at[0, :, kh * DK : (kh + 1) * DK],
                    out_ref.at[d, i * tokens : (i + 1) * tokens],
                    sems.at[len(copies)],
                )
            )
        for i in range(own):
            h = d * own + i
            copies.append(
                pltpu.make_async_copy(
                    v_ref.at[0, :, h * DV : (h + 1) * DV],
                    out_ref.at[d, (keys + i) * tokens : (keys + i + 1) * tokens],
                    sems.at[len(copies)],
                )
            )
    for copy in copies:
        copy.start()
    copies[0].wait()
    copies[1].wait()
    e_scr[...] = jnp.zeros_like(e_scr)
    for which, scr in ((0, g_scr), (1, b_scr)):
        rest = scr[0]
        for part in range(3):
            piece = rest.astype(BF16).astype(F32)
            rest = rest - piece
            for d in range(size):
                at = part * 2 * own + which * own
                e_scr[d, at : at + own] = piece[d * own : (d + 1) * own]
    for d in range(size):
        out_ref[d, (keys + own) * tokens :] = e_scr[d].astype(BF16)
    for copy in copies[2:]:
        copy.wait()


def local_kernel(
    q_ref, k_ref, v_ref, z_ref, g_ref, b_ref, gain_ref, query_ref, intra_ref, gate_ref, d_scr, t_scr
):
    tokens = k_ref.shape[1]
    heads = g_ref.shape[1]
    repeat = heads // (k_ref.shape[2] // DK)
    row, col = row_col(tokens)
    lower = row >= col
    eye = row == col
    gates = g_ref[0]
    betas = b_ref[0]
    tri = jnp.where(lower, 1.0, 0.0)
    cum_cols = dot(tri, gates, NT, HIGH)
    cum_rows = dot(gates, tri, NT, HIGH)
    beta_cols = dot(jnp.where(eye, 1.0, 0.0), betas, NT, HIGH)
    gain = gain_ref[0:1, :]
    key_side = [norms(k_ref[0, :, i * DK : (i + 1) * DK], eye) for i in range(heads // repeat)]
    systems = []
    for h in range(heads):
        gram, key_col, key_row = key_side[h // repeat]
        decay = jnp.exp(jnp.where(row > col, cum_cols[:, h : h + 1] - cum_rows[h : h + 1, :], -1e30))
        systems.append(decay * gram * (beta_cols[:, h : h + 1] * key_col) * key_row)
    found = inverses(systems, d_scr, t_scr)
    for h in range(heads):
        kh = h // repeat
        _, key_col, key_row = key_side[kh]
        key = k_ref[0, :, kh * DK : (kh + 1) * DK]
        if h % repeat == 0:
            query = q_ref[0, :, kh * DK : (kh + 1) * DK]
            queryf = query.astype(F32)
            query_col = lax.rsqrt(jnp.sum(queryf * queryf, axis=1, keepdims=True) + 1e-6) * DK**-0.5
            product = dot(query, key, NT) * query_col * key_row
        scaled = found[h] * betas[h : h + 1, :]
        update = dot(scaled.astype(BF16), v_ref[0, :, h * DV : (h + 1) * DV])
        erase = dot((scaled * (jnp.exp(cum_rows[h : h + 1, :]) * key_row)).astype(BF16), key)
        both = jnp.concatenate([erase, update], axis=1).astype(BF16)
        decay = jnp.exp(jnp.where(lower, cum_cols[:, h : h + 1] - cum_rows[h : h + 1, :], -1e30))
        mixed = dot((decay * product).astype(BF16), both)
        intra_ref[:, h * DV : (h + 1) * DV] = mixed[:, DK:]
        reach = jnp.exp(cum_cols[:, h : h + 1]) * query_col
        query_ref[:, h * DK : (h + 1) * DK] = (reach * queryf - mixed[:, :DK]).astype(BF16)
        z = z_ref[0, :, h * DV : (h + 1) * DV].astype(F32)
        gate_ref[:, h * DV : (h + 1) * DV] = gain * z / (1.0 + jnp.exp(-z))


def group_kernel(own, keys, x_ref, move_ref, add_ref, pair_ref, d_scr, t_scr):
    shards = x_ref.shape[0]
    tokens = DK
    repeat = own // keys
    row, col = row_col(tokens)
    lower = row >= col
    eye = row == col
    base = (keys + own) * tokens
    take_row = lax.broadcasted_iota(jnp.int32, (8, EXTRA), 0)
    take_col = lax.broadcasted_iota(jnp.int32, (8, EXTRA), 1)
    take = jnp.where(
        jnp.logical_and(take_col % (2 * own) == take_row, take_col < 6 * own), 1.0, 0.0
    ).astype(BF16)
    plain = jnp.concatenate([dot(take, x_ref[j, base : base + EXTRA]) for j in range(shards)], axis=0)
    tri = jnp.where(lower, 1.0, 0.0)
    cum_cols = dot(tri, plain, NT, HIGH)
    cum_rows = dot(plain, tri, NT, HIGH)
    plain_cols = dot(jnp.where(eye, 1.0, 0.0), plain, NT, HIGH)

    units = [(j, h) for j in range(shards) for h in range(own)]
    key_side = {}
    for j in range(shards):
        for i in range(keys):
            key_side[j, i] = norms(x_ref[j, i * tokens : (i + 1) * tokens], eye)
    systems = []
    for j, h in units:
        gram, key_col, key_row = key_side[j, h // repeat]
        at = j * 8 + h
        decay = jnp.exp(jnp.where(row > col, cum_cols[:, at : at + 1] - cum_rows[at : at + 1, :], -1e30))
        systems.append(decay * gram * (plain_cols[:, at + own : at + own + 1] * key_col) * key_row)
    found = inverses(systems, d_scr, t_scr)
    rows_at = [j * 8 + h for j, h in units]
    keys_of = [x_ref[j, (h // repeat) * tokens : (h // repeat + 1) * tokens] for j, h in units]
    values_of = [x_ref[j, (keys + h) * tokens : (keys + h + 1) * tokens] for j, h in units]
    sides = [key_side[j, h // repeat] for j, h in units]
    count = range(len(units))
    scaled = [found[u] * plain[rows_at[u] + own : rows_at[u] + own + 1, :] for u in count]
    forward = [jnp.exp(cum_rows[at : at + 1, :]) * side[2] for at, side in zip(rows_at, sides)]
    left = [split(scaled[u]) for u in count]
    right = [split(scaled[u] * forward[u]) for u in count]
    update = [dot(left[u][0], values_of[u]) + dot(left[u][1], values_of[u]) for u in count]
    erase = [dot(right[u][0], keys_of[u]) + dot(right[u][1], keys_of[u]) for u in count]
    lasts = [cum_rows[at : at + 1, tokens - 1 :] for at in rows_at]
    weights = [
        jnp.exp(lasts[u] - cum_cols[:, rows_at[u] : rows_at[u] + 1]) * sides[u][1] for u in count
    ]
    solved = [split(jnp.concatenate([erase[u], update[u]], axis=1) * weights[u]) for u in count]
    both = [dot(keys_of[u], solved[u][0], TN) + dot(keys_of[u], solved[u][1], TN) for u in count]
    moved = {
        units[u]: (jnp.where(eye, jnp.exp(lasts[u]), 0.0) - both[u][:, :DK], both[u][:, DK:])
        for u in count
    }
    start = jnp.concatenate([jnp.where(eye, 1.0, 0.0), jnp.zeros((tokens, DV), F32)], axis=1)
    total = [start for _ in range(own)]
    for j in range(shards):
        for h in range(own):
            move_ref[j, h] = total[h][:, :DK].astype(BF16)
            add_ref[j, h] = total[h][:, DK:]
            gone = dot3(split(moved[j, h][0]), split(total[h]))
            total[h] = jnp.concatenate([gone[:, :DK], gone[:, DK:] + moved[j, h][1]], axis=1)
    for h in range(own):
        pair_ref[h] = total[h].astype(BF16)


def spread(start, final, info_ref, move_ref, add_ref, out_ref):
    size, own = move_ref.shape[0], move_ref.shape[1]
    for h in range(own):
        at = start[h].astype(BF16)
        to = info_ref[1 + h]
        for j in range(size):
            entry = dot(move_ref[j, h], at) + add_ref[j, h]
            kept = jnp.where(to == j, final[h], jnp.zeros_like(final[h]))
            out_ref[j, h] = jnp.concatenate([entry, kept], axis=1).astype(BF16)


def pair_spread_kernel(info_ref, move_ref, add_ref, mine_ref, got_ref, out_ref):
    own = mine_ref.shape[0]
    late = info_ref[0] == 1
    start, final = [], []
    for h in range(own):
        mine, got = mine_ref[h], got_ref[h]
        first = jnp.where(late, got[:, DK:].astype(F32), mine[:, DK:].astype(F32))
        second = jnp.where(late, mine.astype(F32), got.astype(F32))
        final.append(dot(second[:, :DK].astype(BF16), first.astype(BF16)) + second[:, DK:])
        start.append(jnp.where(late, first, jnp.zeros_like(first)))
    spread(start, final, info_ref, move_ref, add_ref, out_ref)


def spread_kernel(info_ref, move_ref, add_ref, start_ref, final_ref, out_ref):
    own = start_ref.shape[0]
    start = [start_ref[h].astype(F32) for h in range(own)]
    final = [final_ref[h].astype(F32) for h in range(own)]
    spread(start, final, info_ref, move_ref, add_ref, out_ref)


def read_kernel(back_ref, query_ref, intra_ref, gate_ref, w_ref, out_ref, q_scr, i_scr, z_scr, w_scr, normed_scr, sems):
    heads = back_ref.shape[0]
    pieces, step = w_scr.shape[0], w_scr.shape[2]
    copies = [
        pltpu.make_async_copy(query_ref, q_scr, sems.at[0]),
        pltpu.make_async_copy(intra_ref, i_scr, sems.at[1]),
        pltpu.make_async_copy(gate_ref, z_scr, sems.at[2]),
    ] + [
        pltpu.make_async_copy(w_ref.at[:, c * step : (c + 1) * step], w_scr.at[c], sems.at[3 + c])
        for c in range(pieces)
    ]
    for copy in copies:
        copy.start()
    for copy in copies[:3]:
        copy.wait()
    for h in range(heads):
        cols = slice(h * DV, (h + 1) * DV)
        value = i_scr[:, cols] + dot(q_scr[:, cols], back_ref[h, :, :DV])
        scale = lax.rsqrt(jnp.mean(value * value, axis=1, keepdims=True) + 1e-6)
        normed_scr[:, cols] = (value * scale * z_scr[:, cols]).astype(BF16)
    for c in range(pieces):
        copies[3 + c].wait()
        out_ref[:, c * step : (c + 1) * step] = dot(normed_scr[...], w_scr[c]).astype(BF16)


def cost(micros):
    return pl.CostEstimate(flops=int(micros * 1.15e9), bytes_accessed=1 << 20, transcendentals=0)


def params(limit=VMEM_LIMIT):
    return pltpu.CompilerParams(vmem_limit_bytes=limit)


def pack(keys, values, log_decay, beta, size):
    tokens, heads, key_heads = keys.shape[1], log_decay.shape[1], keys.shape[2] // DK
    own = heads // size
    carried = max(1, own * key_heads // heads)
    rows = (carried + own) * tokens + EXTRA
    far = pl.BlockSpec(memory_space=pltpu.HBM)
    return pl.pallas_call(
        pack_kernel,
        in_specs=[far, far, far, far],
        out_shape=jax.ShapeDtypeStruct((size, rows, DK), BF16),
        scratch_shapes=[
            pltpu.VMEM(log_decay.shape, F32),
            pltpu.VMEM(beta.shape, F32),
            pltpu.VMEM((size, EXTRA, tokens), F32),
            pltpu.SemaphoreType.DMA((2 + size * (carried + own),)),
        ],
        compiler_params=params(VMEM_MOST),
        cost_estimate=cost(2),
        name="pack",
    )(keys, values, log_decay, beta)


def local_part(queries, keys, values, out_gate, log_decay, beta, gain):
    tokens, heads, key_heads = keys.shape[1], log_decay.shape[1], keys.shape[2] // DK
    step = min(8, heads)
    key_step = step * key_heads // heads
    wide = pl.BlockSpec((tokens, step * DV), lambda i: (0, i))
    narrow = pl.BlockSpec((1, tokens, key_step * DK), lambda i: (0, 0, i))
    broad = pl.BlockSpec((1, tokens, step * DV), lambda i: (0, 0, i))
    thin = pl.BlockSpec((1, step, tokens), lambda i: (0, i, 0))
    return pl.pallas_call(
        local_kernel,
        grid=(heads // step,),
        in_specs=[narrow, narrow, broad, broad, thin, thin, pl.BlockSpec((1, DV), lambda i: (0, 0))],
        out_specs=[wide, wide, wide],
        out_shape=[
            jax.ShapeDtypeStruct((tokens, heads * DK), BF16),
            jax.ShapeDtypeStruct((tokens, heads * DV), F32),
            jax.ShapeDtypeStruct((tokens, heads * DV), F32),
        ],
        scratch_shapes=[pltpu.VMEM((step, tokens, DK), F32), pltpu.VMEM((step, tokens, tokens), F32)],
        compiler_params=params(VMEM_MOST),
        cost_estimate=cost(12),
        name="local_part",
    )(queries, keys, values, out_gate, log_decay, beta, gain)


def group_maps(x, own, keys):
    size = x.shape[0]
    near = pl.BlockSpec(memory_space=pltpu.VMEM)
    return pl.pallas_call(
        lambda *refs: group_kernel(own, keys, *refs),
        in_specs=[near],
        out_specs=[near, near, near],
        out_shape=[
            jax.ShapeDtypeStruct((size, own, DK, DK), BF16),
            jax.ShapeDtypeStruct((size, own, DK, DV), F32),
            jax.ShapeDtypeStruct((own, DK, DK + DV), BF16),
        ],
        scratch_shapes=[
            pltpu.VMEM((size * own, DK, DK), F32),
            pltpu.VMEM((size * own, DK, DK), F32),
        ],
        compiler_params=params(),
        cost_estimate=cost(12),
        name="group_maps",
    )(x)


def spread_states(kernel, info, move, add, one, two):
    near = pl.BlockSpec(memory_space=pltpu.VMEM)
    size, own = move.shape[0], move.shape[1]
    return pl.pallas_call(
        kernel,
        in_specs=[pl.BlockSpec(memory_space=pltpu.SMEM), near, near, near, near],
        out_shape=jax.ShapeDtypeStruct((size, own, DK, 2 * DV), BF16),
        compiler_params=params(),
        cost_estimate=cost(2),
        name="spread_states",
    )(info, move, add, one, two)


def read_out(query, intra, gate, back, weight):
    tokens, width = query.shape
    columns = weight.shape[1]
    pieces = 4
    near = pl.BlockSpec(memory_space=pltpu.VMEM)
    far = pl.BlockSpec(memory_space=pltpu.HBM)
    return pl.pallas_call(
        read_kernel,
        in_specs=[near, far, far, far, far],
        out_shape=jax.ShapeDtypeStruct((tokens, columns), BF16),
        scratch_shapes=[
            pltpu.VMEM(query.shape, query.dtype),
            pltpu.VMEM(intra.shape, intra.dtype),
            pltpu.VMEM(gate.shape, gate.dtype),
            pltpu.VMEM((pieces, width, columns // pieces), BF16),
            pltpu.VMEM((tokens, width), BF16),
            pltpu.SemaphoreType.DMA((3 + pieces,)),
        ],
        compiler_params=params(VMEM_WIDE),
        cost_estimate=cost(4),
        name="read_out",
    )(back, query, intra, gate, weight)


def group_size(count, heads):
    return max(s for s in range(1, 9) if count % s == 0 and heads % s == 0)


def local(queries, keys, values, out_gate, log_decay, beta, norm_gain, out_weight, owner):
    tokens, heads = keys.shape[1], log_decay.shape[1]
    count = lax.axis_size("seq")
    me = lax.axis_index("seq")
    size = group_size(count, heads)
    groups = count // size
    own = heads // size
    carried = max(1, own * (keys.shape[2] // DK) // heads)
    members = [[g * size + i for i in range(size)] for g in range(groups)]

    def swap(x):
        return lax.all_to_all(x, "seq", 0, 0, axis_index_groups=members, tiled=True)

    def hop(x, source, target):
        return lax.ppermute(x, "seq", [(source * size + i, target * size + i) for i in range(size)])

    mine = lax.dynamic_slice_in_dim(owner[0], (me % size) * own, own) - (me // size) * size
    info = jnp.concatenate([(me // size)[None].astype(jnp.int32), mine])

    raw = swap(pack(keys, values, log_decay, beta, size))
    query, intra, gate = local_part(queries, keys, values, out_gate, log_decay, beta, norm_gain[None])
    raw, query, intra, gate = lax.optimization_barrier((raw, query, intra, gate))
    move, add, pair = group_maps(raw, own, carried)
    if groups == 2:
        got = lax.ppermute(pair, "seq", [(i, (i + size) % count) for i in range(count)])
        sent = spread_states(pair_spread_kernel, info, move, add, pair, got)
    else:
        start = jnp.zeros((own, DK, DV), F32)
        wide = pair.astype(F32)

        def leave(start):
            kept = jnp.einsum("hij,hjk->hik", wide[..., :DK], start, precision=HIGH)
            return kept + wide[..., DK:]

        for g in range(groups - 1):
            start = start + hop(leave(start).astype(BF16), g, g + 1).astype(F32)
        last = leave(start).astype(BF16)
        last = jnp.where(me // size == groups - 1, last, jnp.zeros_like(last))
        for g in range(groups - 1, 0, -1):
            last = last + hop(last, g, g - 1)
        sent = spread_states(spread_kernel, info, move, add, start, last)
    back = swap(sent)
    back = back.reshape(heads, DK, 2 * DV)
    decode_states = back[None, :, :, DV:].astype(F32)
    partial_value = read_out(query, intra, gate, back, out_weight)
    ranks = lax.axis_size("head")
    if ranks == 2:
        half = tokens // 2
        rank = lax.axis_index("head")
        keep = lax.dynamic_slice_in_dim(partial_value, rank * half, half)
        give = lax.dynamic_slice_in_dim(partial_value, (1 - rank) * half, half)
        got = lax.ppermute(give, "head", [(0, 1), (1, 0)])
        total = (keep.astype(F32) + got.astype(F32)).astype(BF16)
    else:
        total = lax.psum_scatter(partial_value, "head", scatter_dimension=0, tiled=True)
    return (total[:, None, :], decode_states)


def solution(mesh):
    placed = (
        P(None, "seq", "head"),
        P(None, "seq", "head"),
        P(None, "seq", "head"),
        P(None, "seq", "head"),
        P(None, "head", "seq"),
        P(None, "head", "seq"),
        P(),
        P("head", None),
        P(None, "head"),
    )
    return jax.shard_map(
        local,
        mesh=mesh,
        in_specs=placed,
        out_specs=(P(("seq", "head"), None, None), P("seq", "head", None, None)),
        check_vma=False,
    )
```
